32 devices in a mesh: seq: 4 (over z), head: 2 (over core), dp: 4 (over y, x).
Axes of the slice: x: 2, y: 2, z: 4, core: 2. Of those that a mesh axis runs over, the one named last changes fastest.
Arguments:
- queries: bfloat16 [4, 1024, 16, 128], P('dp', 'seq', 'head'), may hold values from -6 to 6
- keys_in: bfloat16 [4, 1024, 16, 128], P('dp', 'seq', 'head'), may hold values from -6 to 6
- values: bfloat16 [4, 1024, 32, 128], P('dp', 'seq', 'head'), may hold values from -6 to 6
- hidden_in: bfloat16 [4, 1024, 2048], P('dp', 'seq'), may hold values from -6 to 6
- beta_weight: bfloat16 [2048, 32], P(None, 'head'), may hold values from -0.125 to 0.125
- beta_bias: float32 [32], P('head'), may hold values from -4.5 to 1
- log_gate: float32 [4, 1024, 32], P('dp', 'seq', 'head'), may hold values from -0.8 to 0, as said below
- out_grad: bfloat16 [4, 1024, 32, 128], P('dp', 'seq', 'head'), may hold values from -6 to 6
Outputs:
- attended: bfloat16 [4, 1024, 32, 128], P('dp', 'seq', 'head')
- grad_queries: bfloat16 [4, 1024, 16, 128], P('dp', 'seq', 'head')
- grad_keys: bfloat16 [4, 1024, 16, 128], P('dp', 'seq', 'head')
- grad_values: bfloat16 [4, 1024, 32, 128], P('dp', 'seq', 'head')
- grad_log_gate: float32 [4, 1024, 32], P('dp', 'seq', 'head')
- grad_hidden: bfloat16 [4, 1024, 2048], P('dp', 'seq', 'head')
- grad_beta_weight: float32 [2048, 32], P(None, 'head')
The draws below stay inside these ranges and needn't reach their ends.
Inputs may be any that keep to these rules, and one draw needn't show every extreme that they name: log_gate is negative.
All inputs are finite; a program needn't handle non-finite values.
Results may differ from the reference program's by a relative error of at most 0.001.
Values may be sent and summed in bfloat16 or wider, within the bound.
No kernel may reach another device: no remote copies, remote signals or barrier semaphores. Data moves between devices by JAX's collectives and lax.ppermute only.
A program may use at most 192 MiB of HBM per device.

```python
import jax
import jax.numpy as jnp
from jax import lax

D = 2048
HK = 16
VALUE_HEADS = 32
DK = 128
DV = 128
BLOCK = 64
TOK_DEV = 256
BATCH_COUNT = 4
SEQUENCE_LENGTH = 1024
N_SEQ = 4


def head_ranks(key):
    return jax.random.uniform(key, (VALUE_HEADS,))


def draw_beta_bias(key, part):
    ranks = head_ranks(key)
    key = jax.random.fold_in(key, 11)
    random_subkeys = jax.random.split(key, 2)
    slow_share = 0.5
    slow_heads = ranks < slow_share
    slow_bias = jax.random.uniform(random_subkeys[0], (VALUE_HEADS,), minval=-4.5, maxval=-3.5)
    fast_bias = jax.random.uniform(random_subkeys[1], (VALUE_HEADS,), minval=-1.0, maxval=1.0)
    return jnp.where(slow_heads, slow_bias, fast_bias)


def draw_log_gate(key, part):
    ranks = head_ranks(key)
    key = jax.random.fold_in(key, 7)
    random_subkeys = jax.random.split(key, 7)
    slow_share = 0.5
    slow_heads = (ranks < slow_share)[None, None, :]
    slow_rate = jax.random.uniform(random_subkeys[1], (BATCH_COUNT, 1, VALUE_HEADS), minval=0.1, maxval=1.0) / SEQUENCE_LENGTH
    fast_rate = 1.0 / jax.random.uniform(random_subkeys[2], (BATCH_COUNT, 1, VALUE_HEADS), minval=30.0, maxval=50.0)
    baseline_decay_rate = jnp.where(slow_heads, slow_rate, fast_rate)
    partition_multiplier = jnp.exp(jax.random.uniform(random_subkeys[3], (BATCH_COUNT, N_SEQ, 1, VALUE_HEADS), minval=-0.69, maxval=0.69))
    partition_multiplier = jnp.broadcast_to(partition_multiplier, (BATCH_COUNT, N_SEQ, TOK_DEV, VALUE_HEADS)).reshape(BATCH_COUNT, SEQUENCE_LENGTH, VALUE_HEADS)
    jitter_amplitude = jax.random.uniform(random_subkeys[4], (BATCH_COUNT, SEQUENCE_LENGTH, VALUE_HEADS), minval=0.5, maxval=1.5)
    spike_selection = jax.random.uniform(random_subkeys[5], (BATCH_COUNT, SEQUENCE_LENGTH, VALUE_HEADS)) < 3.0 / SEQUENCE_LENGTH
    spike_magnitude = jnp.log(jax.random.uniform(random_subkeys[6], (BATCH_COUNT, SEQUENCE_LENGTH, VALUE_HEADS), minval=0.5, maxval=0.8))
    return -baseline_decay_rate * partition_multiplier * jitter_amplitude + jnp.where(spike_selection, spike_magnitude, 0.0)


def steps_of(stream_key, shape, pieces, smallest, largest):
    def one(position, shards_of):
        steps = jax.random.uniform(jax.random.fold_in(jax.random.fold_in(stream_key, 6), position), (shards_of,), jnp.float32, smallest / len(pieces), largest / len(pieces))
        return jnp.repeat(jnp.exp(steps), shape[position] // shards_of).reshape((-1,) + (1,) * (len(shape) - position - 1))

    loudness = one(*pieces[0])
    for cut in pieces[1:]:
        loudness = loudness * one(*cut)
    return loudness


def bell_draw(key, shape, scale, most, shards=(), kind=jnp.bfloat16):
    gain = steps_of(key, shape, shards, -0.22, 0.18) if shards else 1.0
    entries = jax.random.normal(key, shape, jnp.float32) * scale * gain
    return jnp.minimum(jnp.maximum(entries, -most), most).astype(kind)


def setup_inputs(seed: int = 0) -> dict:
    streams_of = jax.random.split(jax.random.key(seed), 9)
    queries = bell_draw(streams_of[0], (BATCH_COUNT, SEQUENCE_LENGTH, HK, DK), 1.0, 6.0, ((0, 4), (1, 4), (2, 2)))
    keys_in = bell_draw(streams_of[1], (BATCH_COUNT, SEQUENCE_LENGTH, HK, DK), 1.0, 6.0, ((0, 4), (1, 4), (2, 2)))
    values = bell_draw(streams_of[2], (BATCH_COUNT, SEQUENCE_LENGTH, VALUE_HEADS, DV), 1.0, 6.0, ((0, 4), (1, 4), (2, 2)))
    hidden_in = bell_draw(streams_of[3], (BATCH_COUNT, SEQUENCE_LENGTH, D), 1.0, 6.0, ((0, 4), (1, 4)))
    beta_weight = bell_draw(streams_of[4], (D, VALUE_HEADS), D ** -0.5, 0.125, ((1, 2),))
    beta_bias = draw_beta_bias(jax.random.fold_in(streams_of[8], 71), 0)
    log_gate = draw_log_gate(jax.random.fold_in(streams_of[8], 71), 0)
    out_grad = bell_draw(streams_of[7], (BATCH_COUNT, SEQUENCE_LENGTH, VALUE_HEADS, DV), 1.0, 6.0, ((0, 4), (1, 4), (2, 2)))
    return {"queries": queries, "keys_in": keys_in, "values": values, "hidden_in": hidden_in, "beta_weight": beta_weight, "beta_bias": beta_bias, "log_gate": log_gate, "out_grad": out_grad}


eps_norm = 1e-06
highest = lax.Precision.HIGHEST

def unit_rows(tensor, factor):
    return tensor * lax.rsqrt(lax.optimization_barrier(jnp.sum(tensor * tensor, axis=-1, keepdims=True)) + eps_norm) * factor

def recurrence(query_unit, key_unit, value_data, log_rates, beta_gate):
    blocks = SEQUENCE_LENGTH // BLOCK

    def arrange(tensor):
        swapped = jnp.swapaxes(tensor, 0, 1)
        return swapped.reshape((blocks, BLOCK) + swapped.shape[1:])
    sources = (arrange(query_unit), arrange(key_unit), arrange(value_data), arrange(jnp.exp(log_rates)), arrange(beta_gate))

    def token_step(carried, token_items):
        query_tok, key_tok, value_tok, gate_tok, beta_tok = token_items
        predicted = jnp.einsum('bhd,bhde->bhe', key_tok, carried, precision=highest)
        correction = beta_tok[..., None] * (value_tok - gate_tok[..., None] * predicted)
        carried = gate_tok[..., None, None] * carried + key_tok[..., :, None] * correction[..., None, :]
        return (carried, jnp.einsum('bhd,bhde->bhe', query_tok, carried, precision=highest))

    def block_inner(carried, block_items):
        return lax.scan(token_step, carried, block_items)
    block_step = jax.checkpoint(block_inner)
    initial = jnp.zeros((BATCH_COUNT, VALUE_HEADS, DK, DV), jnp.float32)
    _, results = lax.scan(block_step, initial, sources)
    return jnp.swapaxes(results.reshape((SEQUENCE_LENGTH, BATCH_COUNT, VALUE_HEADS, DV)), 0, 1)

def reference(queries, keys_in, values, hidden_in, beta_weight, beta_bias, log_gate, out_grad):
    flat_hidden = hidden_in.reshape(BATCH_COUNT * SEQUENCE_LENGTH, D)
    logits = jnp.dot(flat_hidden, beta_weight, preferred_element_type=jnp.float32).reshape(BATCH_COUNT, SEQUENCE_LENGTH, VALUE_HEADS)
    logits = logits + beta_bias[None, None, :]
    repeats = VALUE_HEADS // HK

    def forward(query_data, key_data, value_data, log_rates, logit_data):
        query_unit = jnp.repeat(unit_rows(query_data, DK ** (-0.5)), repeats, axis=2)
        key_unit = jnp.repeat(unit_rows(key_data, 1.0), repeats, axis=2)
        return recurrence(query_unit, key_unit, value_data, log_rates, jax.nn.sigmoid(logit_data))
    attended, pullback = jax.vjp(forward, queries.astype(jnp.float32), keys_in.astype(jnp.float32), values.astype(jnp.float32), log_gate, logits)
    grad_query, grad_key, grad_value, grad_rates, grad_logits = pullback(out_grad.astype(jnp.float32))
    flat_logits = grad_logits.reshape(BATCH_COUNT * SEQUENCE_LENGTH, VALUE_HEADS)
    grad_weight = jnp.dot(flat_hidden.astype(jnp.float32).T, flat_logits, precision=highest)
    grad_hidden = jnp.dot(flat_logits, beta_weight.astype(jnp.float32).T, precision=highest).reshape(BATCH_COUNT, SEQUENCE_LENGTH, D)
    return (attended.astype(jnp.bfloat16), grad_query.astype(jnp.bfloat16), grad_key.astype(jnp.bfloat16), grad_value.astype(jnp.bfloat16), grad_rates, grad_hidden.astype(jnp.bfloat16), grad_weight)
```

```python
import jax
import jax.numpy as jnp
from jax import lax
from jax.experimental import pallas as pl
from jax.experimental.pallas import tpu as pltpu
from jax.sharding import PartitionSpec as P

SUB = 128
KEY_GROUP = 2
VMEM = 56 * 1024 * 1024

eps_norm = 1e-06
highest = lax.Precision.HIGHEST
f32 = jnp.float32
bf16 = jnp.bfloat16


def split(x):
    high = x.astype(bf16)
    return high, (x - high.astype(f32)).astype(bf16)


def dot(a, b, ca=1, cb=0):
    return lax.dot_general(a, b, (((ca,), (cb,)), ((), ())), preferred_element_type=f32)


def cat(parts, axis):
    return jnp.concatenate(parts, axis=axis)


def halves(x):
    width = x.shape[1] // 2
    return x[:, :width] + x[:, width:]


def square_product(a, b):
    ah, al = split(a)
    bh, bl = split(b)
    wide = cat([bh, bl], 1)
    return halves(dot(cat([ah, al], 1), cat([wide, wide], 0)))


def square_product_t(a, b):
    ah, al = split(a)
    bh, bl = split(b)
    wide = cat([bh, bl], 1)
    return halves(dot(cat([ah, al], 0), cat([wide, wide], 0), 0, 0))


def square_product_bt(a, b):
    ah, al = split(a)
    bh, bl = split(b)
    tall = cat([bh, bl], 0)
    return halves(dot(cat([ah, al], 1), cat([tall, tall], 1), 1, 1))


def positions(count):
    shape = (count, count)
    return (lax.broadcasted_iota(jnp.int32, shape, 0), lax.broadcasted_iota(jnp.int32, shape, 1))


def inverses(blocks):
    count = blocks[0].shape[0]
    row, column = positions(count)
    identity = jnp.where(row == column, 1.0, 0.0)
    found = None
    width = 1
    while width < count:
        pairs = (row // (2 * width) == column // (2 * width)) & (row // width != column // width)
        offs = [jnp.where(pairs, block, 0.0) for block in blocks]
        if found is None:
            found = [identity - off for off in offs]
        else:
            firsts = [square_product(inverse, off) for inverse, off in zip(found, offs)]
            found = [
                inverse - square_product(first, inverse) for first, inverse in zip(firsts, found)
            ]
        width *= 2
    return found


def unit_scales(raw, factor):
    data = raw.astype(f32)
    total = jnp.sum(data * data, axis=1, keepdims=True) + eps_norm
    return lax.rsqrt(total) * factor, total


def as_row(column):
    return jnp.transpose(jnp.broadcast_to(column, (column.shape[0], SUB)))[0:1, :]


def chunk_matrices(kr, qr):
    rk, sk = unit_scales(kr, 1.0)
    rq, sq = unit_scales(qr, kr.shape[1] ** (-0.5))
    rk_row = as_row(rk)
    both = dot(cat([kr, qr], 0), kr, 1, 1) * rk_row
    count = kr.shape[0]
    return rk, sk, rq, sq, rk_row, both[:count] * rk, both[count:] * rq


def decay_matrix(g_col, g_row, lower):
    return jnp.exp(jnp.where(lower, g_col - g_row, -1e30))


def before_kernel(q_ref, k_ref, v_ref, d_ref, rows_ref, cols_ref, t_ref, y_ref, z_ref, m_ref, b_ref, p_ref):
    key_count, count, _ = k_ref.shape
    value_count = v_ref.shape[0]
    share = value_count // key_count
    row, column = positions(count)
    lower = row >= column
    strict = row > column
    rows = rows_ref[0]
    cols = cols_ref[0]
    scales, mixings, systems = [], [], []
    for i in range(key_count):
        kr, qr = k_ref[i], q_ref[i]
        rk, sk, rq, sq, rk_row, key_key, query_key = chunk_matrices(kr, qr)
        for r in range(share):
            h = i * share + r
            g_col, beta = cols[:, h : h + 1], cols[:, value_count + h : value_count + h + 1]
            decay = decay_matrix(g_col, rows[h : h + 1, :], lower)
            systems.append(jnp.where(strict, beta * decay * key_key, 0.0))
            mixings.append(decay * query_key)
            scales.append((rk, rq, beta, g_col))
    pieces = count // SUB
    diagonal = []
    for a in systems:
        for n in range(pieces):
            diagonal.append(a[n * SUB : (n + 1) * SUB, n * SUB : (n + 1) * SUB])
    diagonal = inverses(diagonal)
    identity = jnp.where(positions(SUB)[0] == positions(SUB)[1], 1.0, 0.0)
    for h in range(value_count):
        a = systems[h]
        blocks = [[None] * pieces for _ in range(pieces)]
        for n in range(pieces):
            blocks[n][n] = diagonal[h * pieces + n]
            for m in range(n):
                total = None
                for l in range(m, n):
                    term = square_product(
                        a[n * SUB : (n + 1) * SUB, l * SUB : (l + 1) * SUB], blocks[l][m]
                    )
                    total = term if total is None else total + term
                blocks[n][m] = -square_product(blocks[n][n], total)
            for m in range(n + 1, pieces):
                blocks[n][m] = jnp.zeros((SUB, SUB), f32)
        inverse = cat([cat(line, 1) for line in blocks], 0)
        rk, rq, beta, g_col = scales[h]
        kr, qr, v, d = k_ref[h // share], q_ref[h // share], v_ref[h], d_ref[h]
        width = kr.shape[1]
        last = g_col[count - 1 : count, :]
        growth = jnp.exp(g_col)
        to_end = jnp.exp(last - g_col) * rk
        ph, pl_ = split(mixings[h])
        pulled = dot(ph, d, 0, 0) + dot(pl_, d, 0, 0)
        th, tl = split(inverse)
        keys_h, keys_l = split(to_end * kr.astype(f32))
        pull_h, pull_l = split(pulled)
        high = dot(th, cat([keys_h, pull_h, keys_l, pull_l], 1), 0, 0)
        yz = high[:, : 2 * width] + high[:, 2 * width :]
        yz = yz + dot(tl, cat([keys_h, pull_h], 1), 0, 0)
        y, z = yz[:, :width], yz[:, width:]
        t_ref[h] = inverse
        y_ref[h] = y
        z_ref[h] = z
        yb = y * beta
        bh, bl = split(yb)
        b_ref[h] = dot(bh, v, 0, 0) + dot(bl, v, 0, 0)
        mh, ml = split(yb * (growth * rk))
        m_ref[h] = identity * jnp.exp(last) - (dot(mh, kr, 0, 0) + dot(ml, kr, 0, 0))
        outs_h, outs_l = split((growth * rq) * d.astype(f32))
        ins_h, ins_l = split((beta * growth * rk) * z)
        p_ref[h] = halves(
            dot(qr, cat([outs_h, outs_l], 1), 0, 0) - dot(kr, cat([ins_h, ins_l], 1), 0, 0)
        )


def relay_kernel(m_ref, b_ref, p_ref, s_ref, e_ref, so_ref, eo_ref):
    for h in range(m_ref.shape[0]):
        m = m_ref[h]
        so_ref[h] = square_product(m, s_ref[h]) + b_ref[h]
        eo_ref[h] = square_product_t(m, e_ref[h]) + p_ref[h]


def after_kernel(
    q_ref, k_ref, v_ref, d_ref, rows_ref, cols_ref, t_ref, y_ref, z_ref, s_ref, e_ref,
    o_ref, dq_ref, dk_ref, dv_ref, small_ref,
):
    key_count, count, width = k_ref.shape
    value_count = v_ref.shape[0]
    share = value_count // key_count
    row, column = positions(count)
    lower = row >= column
    strict = row > column
    rows = rows_ref[0]
    cols = cols_ref[0]
    gates, logits = [], []
    for i in range(key_count):
        kr, qr = k_ref[i], q_ref[i]
        kf, qf = kr.astype(f32), qr.astype(f32)
        rk, sk, rq, sq, rk_row, key_key, query_key = chunk_matrices(kr, qr)
        both = cat([qr, kr], 0)
        mix_grad = pair_grad = dq = dk = None
        for r in range(share):
            h = i * share + r
            g_col, beta = cols[:, h : h + 1], cols[:, value_count + h : value_count + h + 1]
            decay = decay_matrix(g_col, rows[h : h + 1, :], lower)
            growth = jnp.exp(g_col)
            last = g_col[count - 1 : count, :]
            to_end = jnp.exp(last - g_col)
            v, d = v_ref[h], d_ref[h]
            vf, df = v.astype(f32), d.astype(f32)
            s, e = s_ref[h], e_ref[h]
            sh, sl = split(s)
            eh, el = split(e)
            carried = halves(dot(both, cat([sh, sl], 1)))
            residual = beta * (vf - (growth * rk) * carried[count:])
            rh, rl = split(residual)
            th, tl = split(t_ref[h])
            new = halves(dot(th, cat([rh, rl], 1))) + dot(tl, rh)
            nh, nl = split(new)
            ph, pl_ = split(decay * query_key)
            out = (growth * rq) * carried[:count] + halves(dot(ph, cat([nh, nl], 1))) + dot(pl_, nh)
            o_ref[h] = out.astype(bf16)
            d_res = z_ref[h] + square_product(y_ref[h], e)
            dv = beta * d_res
            dv_ref[h] = dv.astype(bf16)
            logits.append((1.0 - beta) * jnp.sum(d_res * new, axis=1, keepdims=True))
            gate = jnp.sum(df * out - dv * vf, axis=1, keepdims=True)
            drh, drl = split(d_res)
            tall = cat([nh, nl], 1)
            d_mix = dot(cat([d, d], 1), tall, 1, 1)
            d_sys = dot(cat([drh, drh], 1), tall, 1, 1) + dot(drl, nh, 1, 1)
            term = decay * d_mix
            mix_grad = term if mix_grad is None else mix_grad + term
            term = jnp.where(strict, beta * decay * d_sys, 0.0)
            pair_grad = term if pair_grad is None else pair_grad + term
            term = growth * dot(cat([d, d], 1), cat([sh, sl], 1), 1, 1)
            dq = term if dq is None else dq + term
            from_end = to_end * square_product_bt(new, e)
            from_in = (growth * beta) * square_product_bt(d_res, s)
            total = jnp.sum(from_end * kf * rk, axis=0, keepdims=True) + jnp.exp(last) * jnp.sum(
                s * e, axis=0, keepdims=True
            )
            total = jnp.sum(total, axis=1, keepdims=True)
            at_end = lax.broadcasted_iota(jnp.int32, (count, 1), 0) == count - 1
            gates.append(gate + jnp.where(at_end, total, 0.0))
            term = from_end - from_in
            dk = term if dk is None else dk + term
        mh, ml = split(mix_grad * rk_row)
        dq = dq + dot(mh, kr) + dot(ml, kr)
        xh, xl = split(mix_grad * rq)
        dk = dk + dot(xh, qr, 0, 0) + dot(xl, qr, 0, 0)
        gh, gl = split(pair_grad * rk_row)
        dk = dk - (dot(gh, kr) + dot(gl, kr))
        gh, gl = split(pair_grad * rk)
        dk = dk - (dot(gh, kr, 0, 0) + dot(gl, kr, 0, 0))
        along = jnp.sum(qf * dq, axis=1, keepdims=True)
        dq_ref[i] = (rq * (dq - qf * (along / sq))).astype(bf16)
        along = jnp.sum(kf * dk, axis=1, keepdims=True)
        dk_ref[i] = (rk * (dk - kf * (along / sk))).astype(bf16)
    small_ref[0] = cat(gates + logits, 1)


def leading(shape, group, index):
    return pl.BlockSpec((group,) + shape[1:], lambda step: (index,) + (0,) * (len(shape) - 1))


def call(kernel, name, operands, groups, outs, flops):
    return pl.pallas_call(
        kernel,
        name=name,
        grid=(1,),
        in_specs=[leading(x.shape, size, index) for x, (size, index) in zip(operands, groups)],
        out_specs=[leading(shape, shape[0], 0) for shape, _ in outs],
        out_shape=[jax.ShapeDtypeStruct(shape, kind) for shape, kind in outs],
        compiler_params=pltpu.CompilerParams(vmem_limit_bytes=VMEM),
        cost_estimate=pl.CostEstimate(flops=flops, bytes_accessed=1 << 20, transcendentals=0),
    )(*operands)


def on_device(queries, keys_in, values, hidden_in, beta_weight, beta_bias, log_gate, out_grad):
    batches, tokens, model_width = hidden_in.shape
    key_heads, key_dim = queries.shape[2:]
    value_heads, value_dim = values.shape[2:]
    share = value_heads // key_heads
    count = lax.axis_size("seq")

    flat_hidden = hidden_in.reshape(batches * tokens, model_width)
    logits = jnp.dot(flat_hidden, beta_weight, preferred_element_type=f32)
    logits = logits.reshape(batches, tokens, value_heads) + beta_bias[None, None, :]
    beta = jax.nn.sigmoid(logits)
    summed = jnp.cumsum(log_gate, axis=1)

    def by_head(x):
        return jnp.swapaxes(x, 1, 2).reshape(-1, tokens, x.shape[3])

    q, k, v, d = by_head(queries), by_head(keys_in), by_head(values), by_head(out_grad)
    nk = KEY_GROUP
    nv = nk * share
    parts = batches * key_heads // nk
    rows = jnp.swapaxes(jnp.stack([summed, beta], 0), 2, 3)
    rows = rows.reshape(2, parts, nv, tokens).swapaxes(0, 1).reshape(parts, 2 * nv, tokens)
    cols = jnp.swapaxes(rows, 1, 2)

    state = (nv, key_dim, value_dim)
    chunk = (nv, tokens, value_dim)
    befores = []
    for part in range(parts):
        befores.append(
            call(
                before_kernel, "before", (q, k, v, d, rows, cols),
                ((nk, part), (nk, part), (nv, part), (nv, part), (1, part), (1, part)),
                (((nv, tokens, tokens), f32), (chunk, f32), (chunk, f32), (state, f32), (state, f32), (state, f32)),
                nv * 60 * 2 * tokens**3,
            )
        )
    ins = [jnp.zeros(state, f32) for _ in range(parts)]
    exits = [jnp.zeros(state, f32) for _ in range(parts)]
    sends = [(b[4], b[5]) for b in befores]
    for hop in range(count - 1):
        for part in range(parts):
            if hop:
                sends[part] = call(
                    relay_kernel, "relay", [*befores[part][3:], ins[part], exits[part]],
                    ((nv, 0),) * 5, ((state, f32), (state, f32)), nv * 8 * 2 * key_dim**3,
                )
            onward = lax.ppermute(sends[part][0], "seq", [(hop, hop + 1)])
            back = lax.ppermute(sends[part][1], "seq", [(count - 1 - hop, count - 2 - hop)])
            ins[part] = ins[part] + onward
            exits[part] = exits[part] + back
    afters = []
    for part in range(parts):
        t, y, z = befores[part][:3]
        afters.append(
            call(
                after_kernel, "after", (q, k, v, d, rows, cols, t, y, z, ins[part], exits[part]),
                ((nk, part), (nk, part), (nv, part), (nv, part), (1, part), (1, part)) + ((nv, 0),) * 5,
                (
                    (chunk, bf16), ((nk, tokens, key_dim), bf16), ((nk, tokens, key_dim), bf16),
                    (chunk, bf16), ((1, tokens, 2 * nv), f32),
                ),
                nv * 40 * 2 * tokens**3,
            )
        )

    def by_token(index, heads):
        whole = jnp.concatenate([a[index] for a in afters], 0)
        return jnp.swapaxes(whole.reshape(batches, heads, tokens, whole.shape[2]), 1, 2)

    def small(first):
        parts_of = jnp.stack([a[4][0, :, first : first + nv] for a in afters], 1)
        return jnp.swapaxes(parts_of.reshape(tokens, batches, value_heads), 0, 1)

    grad_gate = lax.cumsum(small(0), axis=1, reverse=True)
    grad_logits = small(nv).reshape(batches * tokens, value_heads)
    weight_part = jnp.dot(flat_hidden.astype(f32).T, grad_logits, precision=highest)
    grad_weight = lax.psum(weight_part, ("seq", "dp"))
    all_logits = lax.all_gather(grad_logits, "head", axis=1, tiled=True)
    all_weight = lax.all_to_all(beta_weight, "head", 0, 1, tiled=True)
    grad_hidden = jnp.dot(all_logits, all_weight.astype(f32).T, precision=highest)
    return (
        by_token(0, value_heads),
        by_token(1, key_heads),
        by_token(2, key_heads),
        by_token(3, value_heads),
        grad_gate,
        grad_hidden.astype(bf16).reshape(batches, tokens, -1),
        grad_weight,
    )


def solution(mesh):
    heads = P("dp", "seq", "head", None)
    return jax.shard_map(
        on_device,
        mesh=mesh,
        in_specs=(
            heads, heads, heads, P("dp", "seq", None), P(None, "head"), P("head"),
            P("dp", "seq", "head"), heads,
        ),
        out_specs=(
            heads, heads, heads, heads, P("dp", "seq", "head"), P("dp", "seq", "head"), P(None, "head"),
        ),
        check_vma=False,
    )
```

```python
import functools

import jax
import jax.numpy as jnp
from jax import lax
from jax.experimental import pallas as pl
from jax.experimental.pallas import tpu as pltpu
from jax.sharding import PartitionSpec as P

SUB = 128
KEY_GROUP = 2
VMEM = 56 * 1024 * 1024

eps_norm = 1e-06
highest = lax.Precision.HIGHEST
f32 = jnp.float32
bf16 = jnp.bfloat16


def split(x):
    high = x.astype(bf16)
    return high, (x - high.astype(f32)).astype(bf16)


def dot(a, b, ca=1, cb=0):
    return lax.dot_general(a, b, (((ca,), (cb,)), ((), ())), preferred_element_type=f32)


def cat(parts, axis):
    return jnp.concatenate(parts, axis=axis)


def halves(x):
    width = x.shape[1] // 2
    return x[:, :width] + x[:, width:]


def square_product(a, b):
    ah, al = split(a)
    bh, bl = split(b)
    wide = cat([bh, bl], 1)
    return halves(dot(cat([ah, al], 1), cat([wide, wide], 0)))


def square_product_t(a, b):
    ah, al = split(a)
    bh, bl = split(b)
    wide = cat([bh, bl], 1)
    return halves(dot(cat([ah, al], 0), cat([wide, wide], 0), 0, 0))


def square_product_bt(a, b):
    ah, al = split(a)
    bh, bl = split(b)
    tall = cat([bh, bl], 0)
    return halves(dot(cat([ah, al], 1), cat([tall, tall], 1), 1, 1))


def positions(count):
    shape = (count, count)
    return (lax.broadcasted_iota(jnp.int32, shape, 0), lax.broadcasted_iota(jnp.int32, shape, 1))


def inverses(blocks):
    count = blocks[0].shape[0]
    row, column = positions(count)
    identity = jnp.where(row == column, 1.0, 0.0)
    found = None
    width = 1
    while width < count:
        pairs = (row // (2 * width) == column // (2 * width)) & (row // width != column // width)
        offs = [jnp.where(pairs, block, 0.0) for block in blocks]
        if found is None:
            found = [identity - off for off in offs]
        else:
            firsts = [square_product(inverse, off) for inverse, off in zip(found, offs)]
            found = [
                inverse - square_product(first, inverse) for first, inverse in zip(firsts, found)
            ]
        width *= 2
    return found


def unit_scales(raw, factor):
    data = raw.astype(f32)
    total = jnp.sum(data * data, axis=1, keepdims=True) + eps_norm
    return lax.rsqrt(total) * factor, total


def as_row(column):
    return jnp.transpose(jnp.broadcast_to(column, (column.shape[0], SUB)))[0:1, :]


def chunk_matrices(kr, qr):
    rk, sk = unit_scales(kr, 1.0)
    rq, sq = unit_scales(qr, kr.shape[1] ** (-0.5))
    rk_row = as_row(rk)
    both = dot(cat([kr, qr], 0), kr, 1, 1) * rk_row
    count = kr.shape[0]
    return rk, sk, rq, sq, rk_row, both[:count] * rk, both[count:] * rq


def decay_matrix(g_col, g_row, lower):
    return jnp.exp(jnp.where(lower, g_col - g_row, -1e30))


def before_kernel(
    place_ref, q_ref, k_ref, v_ref, d_ref, rows_ref, cols_ref,
    t_ref, y_ref, z_ref, m_ref, b_ref, p_ref, first_ref,
):
    key_count, count, _ = k_ref.shape
    value_count = v_ref.shape[0]
    share = value_count // key_count
    row, column = positions(count)
    lower = row >= column
    strict = row > column
    rows = rows_ref[0]
    cols = cols_ref[0]
    scales, mixings, systems = [], [], []
    for i in range(key_count):
        kr, qr = k_ref[i], q_ref[i]
        rk, sk, rq, sq, rk_row, key_key, query_key = chunk_matrices(kr, qr)
        for r in range(share):
            h = i * share + r
            g_col, beta = cols[:, h : h + 1], cols[:, value_count + h : value_count + h + 1]
            decay = decay_matrix(g_col, rows[h : h + 1, :], lower)
            systems.append(jnp.where(strict, beta * decay * key_key, 0.0))
            mixings.append(decay * query_key)
            scales.append((rk, rq, beta, g_col))
    pieces = count // SUB
    diagonal = []
    for a in systems:
        for n in range(pieces):
            diagonal.append(a[n * SUB : (n + 1) * SUB, n * SUB : (n + 1) * SUB])
    diagonal = inverses(diagonal)
    identity = jnp.where(positions(SUB)[0] == positions(SUB)[1], 1.0, 0.0)
    for h in range(value_count):
        a = systems[h]
        blocks = [[None] * pieces for _ in range(pieces)]
        for n in range(pieces):
            blocks[n][n] = diagonal[h * pieces + n]
            for m in range(n):
                total = None
                for l in range(m, n):
                    term = square_product(
                        a[n * SUB : (n + 1) * SUB, l * SUB : (l + 1) * SUB], blocks[l][m]
                    )
                    total = term if total is None else total + term
                blocks[n][m] = -square_product(blocks[n][n], total)
            for m in range(n + 1, pieces):
                blocks[n][m] = jnp.zeros((SUB, SUB), f32)
        inverse = cat([cat(line, 1) for line in blocks], 0)
        rk, rq, beta, g_col = scales[h]
        kr, qr, v, d = k_ref[h // share], q_ref[h // share], v_ref[h], d_ref[h]
        width = kr.shape[1]
        last = g_col[count - 1 : count, :]
        growth = jnp.exp(g_col)
        to_end = jnp.exp(last - g_col) * rk
        ph, pl_ = split(mixings[h])
        pulled = dot(ph, d, 0, 0) + dot(pl_, d, 0, 0)
        th, tl = split(inverse)
        keys_h, keys_l = split(to_end * kr.astype(f32))
        pull_h, pull_l = split(pulled)
        high = dot(th, cat([keys_h, pull_h, keys_l, pull_l], 1), 0, 0)
        yz = high[:, : 2 * width] + high[:, 2 * width :]
        yz = yz + dot(tl, cat([keys_h, pull_h], 1), 0, 0)
        y, z = yz[:, :width], yz[:, width:]
        t_ref[h] = inverse
        y_ref[h] = y
        z_ref[h] = z
        yb = y * beta
        bh, bl = split(yb)
        base = dot(bh, v, 0, 0) + dot(bl, v, 0, 0)
        mh, ml = split(yb * (growth * rk))
        m_ref[h] = identity * jnp.exp(last) - (dot(mh, kr, 0, 0) + dot(ml, kr, 0, 0))
        outs_h, outs_l = split((growth * rq) * d.astype(f32))
        ins_h, ins_l = split((beta * growth * rk) * z)
        push = halves(
            dot(qr, cat([outs_h, outs_l], 1), 0, 0) - dot(kr, cat([ins_h, ins_l], 1), 0, 0)
        )
        b_ref[h] = base
        p_ref[h] = push
        first_ref[h] = jnp.where(place_ref[0] == 0, base, push)


def relay_kernel(hop, count, place_ref, m_ref, b_ref, p_ref, got_ref, out_ref):
    place = place_ref[0]

    @pl.when(place == hop)
    def _():
        for h in range(m_ref.shape[0]):
            out_ref[h] = square_product(m_ref[h], got_ref[h]) + b_ref[h]

    @pl.when(place == count - 1 - hop)
    def _():
        for h in range(m_ref.shape[0]):
            out_ref[h] = square_product_t(m_ref[h], got_ref[h]) + p_ref[h]


def chosen(place, arrivals, h, first, step):
    total = jnp.zeros(arrivals[0].shape[1:], f32)
    for hop, arrival in enumerate(arrivals):
        total = jnp.where(first + step * place == hop, arrival[h], total)
    return total


def values_kernel(*refs):
    place_ref, q_ref, k_ref, v_ref, d_ref, rows_ref, cols_ref, t_ref, y_ref, z_ref = refs[:10]
    arrivals = refs[10:-7]
    o_ref, dv_ref, n_ref, r_ref, s_ref, e_ref, small_ref = refs[-7:]
    key_count, count, width = k_ref.shape
    value_count = v_ref.shape[0]
    share = value_count // key_count
    row, column = positions(count)
    lower = row >= column
    rows = rows_ref[0]
    cols = cols_ref[0]
    place = place_ref[0]
    gates, logits = [], []
    for i in range(key_count):
        kr, qr = k_ref[i], q_ref[i]
        rk, _ = unit_scales(kr, 1.0)
        rq, _ = unit_scales(qr, width ** (-0.5))
        query_key = dot(qr, kr, 1, 1) * as_row(rk) * rq
        both = cat([qr, kr], 0)
        for r in range(share):
            h = i * share + r
            g_col, beta = cols[:, h : h + 1], cols[:, value_count + h : value_count + h + 1]
            decay = decay_matrix(g_col, rows[h : h + 1, :], lower)
            growth = jnp.exp(g_col)
            v, d = v_ref[h], d_ref[h]
            vf, df = v.astype(f32), d.astype(f32)
            s = chosen(place, arrivals, h, -1, 1)
            e = chosen(place, arrivals, h, len(arrivals) - 1, -1)
            s_ref[h] = s
            e_ref[h] = e
            sh, sl = split(s)
            carried = halves(dot(both, cat([sh, sl], 1)))
            residual = beta * (vf - (growth * rk) * carried[count:])
            rh, rl = split(residual)
            th, tl = split(t_ref[h])
            new = halves(dot(th, cat([rh, rl], 1))) + dot(tl, rh)
            n_ref[h] = new
            nh, nl = split(new)
            ph, pl_ = split(decay * query_key)
            out = (growth * rq) * carried[:count] + halves(dot(ph, cat([nh, nl], 1))) + dot(pl_, nh)
            o_ref[h] = out.astype(bf16)
            d_res = z_ref[h] + square_product(y_ref[h], e)
            r_ref[h] = d_res
            dv = beta * d_res
            dv_ref[h] = dv.astype(bf16)
            logits.append((1.0 - beta) * jnp.sum(d_res * new, axis=1, keepdims=True))
            gates.append(jnp.sum(df * out - dv * vf, axis=1, keepdims=True))
    after = jnp.where(row <= column, 1.0, 0.0).astype(bf16)
    gh, gl = split(cat(gates, 1))
    small_ref[0] = cat([halves(dot(after, cat([gh, gl], 1)))] + logits, 1)


def keys_kernel(
    q_ref, k_ref, d_ref, rows_ref, cols_ref, n_ref, r_ref, s_ref, e_ref, small_ref,
    dq_ref, dk_ref, gate_ref,
):
    key_count, count, width = k_ref.shape
    value_count = d_ref.shape[0]
    share = value_count // key_count
    row, column = positions(count)
    lower = row >= column
    strict = row > column
    rows = rows_ref[0]
    cols = cols_ref[0]
    gates = []
    for i in range(key_count):
        kr, qr = k_ref[i], q_ref[i]
        kf, qf = kr.astype(f32), qr.astype(f32)
        rk, sk = unit_scales(kr, 1.0)
        rq, sq = unit_scales(qr, width ** (-0.5))
        rk_row = as_row(rk)
        mix_grad = pair_grad = dq = dk = None
        for r in range(share):
            h = i * share + r
            g_col, beta = cols[:, h : h + 1], cols[:, value_count + h : value_count + h + 1]
            decay = decay_matrix(g_col, rows[h : h + 1, :], lower)
            growth = jnp.exp(g_col)
            last = g_col[count - 1 : count, :]
            to_end = jnp.exp(last - g_col)
            d = d_ref[h]
            s, e, new, d_res = s_ref[h], e_ref[h], n_ref[h], r_ref[h]
            sh, sl = split(s)
            nh, nl = split(new)
            drh, drl = split(d_res)
            tall = cat([nh, nl], 1)
            d_mix = dot(cat([d, d], 1), tall, 1, 1)
            d_sys = dot(cat([drh, drh], 1), tall, 1, 1) + dot(drl, nh, 1, 1)
            term = decay * d_mix
            mix_grad = term if mix_grad is None else mix_grad + term
            term = jnp.where(strict, beta * decay * d_sys, 0.0)
            pair_grad = term if pair_grad is None else pair_grad + term
            term = growth * dot(cat([d, d], 1), cat([sh, sl], 1), 1, 1)
            dq = term if dq is None else dq + term
            from_end = to_end * square_product_bt(new, e)
            from_in = (growth * beta) * square_product_bt(d_res, s)
            total = jnp.sum(from_end * kf * rk, axis=0, keepdims=True) + jnp.exp(last) * jnp.sum(
                s * e, axis=0, keepdims=True
            )
            gates.append(jnp.sum(total, axis=1, keepdims=True))
            term = from_end - from_in
            dk = term if dk is None else dk + term
        mh, ml = split(mix_grad * rk_row)
        dq = dq + dot(mh, kr) + dot(ml, kr)
        xh, xl = split(mix_grad * rq)
        dk = dk + dot(xh, qr, 0, 0) + dot(xl, qr, 0, 0)
        gh, gl = split(pair_grad * rk_row)
        dk = dk - (dot(gh, kr) + dot(gl, kr))
        gh, gl = split(pair_grad * rk)
        dk = dk - (dot(gh, kr, 0, 0) + dot(gl, kr, 0, 0))
        along = jnp.sum(qf * dq, axis=1, keepdims=True)
        dq_ref[i] = (rq * (dq - qf * (along / sq))).astype(bf16)
        along = jnp.sum(kf * dk, axis=1, keepdims=True)
        dk_ref[i] = (rk * (dk - kf * (along / sk))).astype(bf16)
    gate_ref[0] = small_ref[0][:, :value_count] + cat(gates, 1)


def leading(shape, group, index):
    return pl.BlockSpec((group,) + shape[1:], lambda step: (index,) + (0,) * (len(shape) - 1))


def call(kernel, name, operands, groups, outs, flops):
    return pl.pallas_call(
        kernel,
        name=name,
        grid=(1,),
        in_specs=[
            pl.BlockSpec(memory_space=pltpu.SMEM) if part is None else leading(x.shape, *part)
            for x, part in zip(operands, groups)
        ],
        out_specs=[leading(shape, shape[0], 0) for shape, _ in outs],
        out_shape=[jax.ShapeDtypeStruct(shape, kind) for shape, kind in outs],
        compiler_params=pltpu.CompilerParams(vmem_limit_bytes=VMEM),
        cost_estimate=pl.CostEstimate(flops=flops, bytes_accessed=1 << 20, transcendentals=0),
    )(*operands)


def total_over(value, axes):
    for axis in axes:
        step = 1
        while step < lax.axis_size(axis):
            pairs = [(i, i ^ step) for i in range(lax.axis_size(axis))]
            value = value + lax.ppermute(value, axis, pairs)
            step *= 2
    return value


def on_device(queries, keys_in, values, hidden_in, beta_weight, beta_bias, log_gate, out_grad):
    batches, tokens, model_width = hidden_in.shape
    key_heads, key_dim = queries.shape[2:]
    value_heads, value_dim = values.shape[2:]
    share = value_heads // key_heads
    count = lax.axis_size("seq")

    flat_hidden = hidden_in.reshape(batches * tokens, model_width)
    logits = jnp.dot(flat_hidden, beta_weight, preferred_element_type=f32)
    logits = logits.reshape(batches, tokens, value_heads) + beta_bias[None, None, :]
    beta = jax.nn.sigmoid(logits)
    summed = jnp.cumsum(log_gate, axis=1)

    def by_head(x):
        return jnp.swapaxes(x, 1, 2).reshape(-1, tokens, x.shape[3])

    q, k, v, d = by_head(queries), by_head(keys_in), by_head(values), by_head(out_grad)
    nk = KEY_GROUP
    nv = nk * share
    parts = batches * key_heads // nk
    rows = jnp.swapaxes(jnp.stack([summed, beta], 0), 2, 3)
    rows = rows.reshape(2, parts, nv, tokens).swapaxes(0, 1).reshape(parts, 2 * nv, tokens)
    cols = jnp.swapaxes(rows, 1, 2)

    state = (nv, key_dim, value_dim)
    chunk = (nv, tokens, value_dim)
    place = lax.axis_index("seq").astype(jnp.int32).reshape(1)
    befores = []
    for part in range(parts):
        befores.append(
            call(
                before_kernel, "before", (place, q, k, v, d, rows, cols),
                (None, (nk, part), (nk, part), (nv, part), (nv, part), (1, part), (1, part)),
                (((nv, tokens, tokens), f32), (chunk, f32), (chunk, f32)) + ((state, f32),) * 4,
                nv * 60 * 2 * tokens**3,
            )
        )
    sends = [b[6] for b in befores]
    arrivals = [[] for _ in range(parts)]
    for hop in range(count - 1):
        for part in range(parts):
            if hop:
                (sends[part],) = call(
                    functools.partial(relay_kernel, hop, count), "relay",
                    (place, *befores[part][3:6], arrivals[part][-1]),
                    (None,) + ((nv, 0),) * 4, ((state, f32),), nv * 8 * 2 * key_dim**3,
                )
            route = [(hop, hop + 1), (count - 1 - hop, count - 2 - hop)]
            arrivals[part].append(lax.ppermute(sends[part], "seq", route))
    firsts = []
    for part in range(parts):
        t, y, z = befores[part][:3]
        firsts.append(
            call(
                values_kernel, "values", (place, q, k, v, d, rows, cols, t, y, z, *arrivals[part]),
                (None, (nk, part), (nk, part), (nv, part), (nv, part), (1, part), (1, part))
                + ((nv, 0),) * (3 + len(arrivals[part])),
                (
                    (chunk, bf16), (chunk, bf16), (chunk, f32), (chunk, f32), (state, f32), (state, f32),
                    ((1, tokens, 2 * nv), f32),
                ),
                nv * 20 * 2 * tokens**3,
            )
        )
    seconds = []
    for part in range(parts):
        _, _, n, r, s, e, small = firsts[part]
        narrow = ((nk, tokens, key_dim), bf16)
        seconds.append(
            call(
                keys_kernel, "keys", (q, k, d, rows, cols, n, r, s, e, small),
                ((nk, part), (nk, part), (nv, part), (1, part), (1, part)) + ((nv, 0),) * 4 + ((1, 0),),
                (narrow, narrow, ((1, tokens, nv), f32)),
                nv * 20 * 2 * tokens**3,
            )
        )

    def by_token(results, heads):
        whole = jnp.concatenate(results, 0)
        return jnp.swapaxes(whole.reshape(batches, heads, tokens, whole.shape[2]), 1, 2)

    def small_array(results):
        parts_of = jnp.stack(results, 1)
        return jnp.swapaxes(parts_of.reshape(tokens, batches, value_heads), 0, 1)

    grad_gate = small_array([a[2][0] for a in seconds])
    grad_logits = small_array([a[6][0, :, nv:] for a in firsts]).reshape(batches * tokens, value_heads)
    weight_part = jnp.dot(grad_logits.T, flat_hidden.astype(f32), precision=highest)
    grad_weight = total_over(weight_part, ("dp", "seq")).T
    here = lax.axis_index("head")
    half = model_width // 2
    weight_here = lax.dynamic_slice_in_dim(beta_weight, here * half, half, 0)
    weight_there = lax.dynamic_slice_in_dim(beta_weight, (1 - here) * half, half, 0)
    swap = [(0, 1), (1, 0)]
    all_weight = jnp.concatenate([weight_here, lax.ppermute(weight_there, "head", swap)], 1)
    all_logits = jnp.concatenate([grad_logits, lax.ppermute(grad_logits, "head", swap)], 1)
    grad_hidden = jnp.dot(all_logits, all_weight.astype(f32).T, precision=highest)
    return (
        by_token([a[0] for a in firsts], value_heads),
        by_token([a[0] for a in seconds], key_heads),
        by_token([a[1] for a in seconds], key_heads),
        by_token([a[1] for a in firsts], value_heads),
        grad_gate,
        grad_hidden.astype(bf16).reshape(batches, tokens, -1),
        grad_weight,
    )


def solution(mesh):
    heads = P("dp", "seq", "head", None)
    return jax.shard_map(
        on_device,
        mesh=mesh,
        in_specs=(
            heads, heads, heads, P("dp", "seq", None), P(None, "head"), P("head"),
            P("dp", "seq", "head"), heads,
        ),
        out_specs=(
            heads, heads, heads, heads, P("dp", "seq", "head"), P("dp", "seq", "head"), P(None, "head"),
        ),
        check_vma=False,
    )
```

```python
import functools

import jax
import jax.numpy as jnp
from jax import lax
from jax.experimental import pallas as pl
from jax.experimental.pallas import tpu as pltpu
from jax.sharding import PartitionSpec as P

SUB = 128
KEY_GROUP = 2
VMEM = 24 * 1024 * 1024

eps_norm = 1e-06
f32 = jnp.float32
bf16 = jnp.bfloat16


def split(x):
    high = x.astype(bf16)
    return high, (x - high.astype(f32)).astype(bf16)


def dot(a, b, ca=1, cb=0):
    return lax.dot_general(a, b, (((ca,), (cb,)), ((), ())), preferred_element_type=f32)


def cat(parts, axis):
    return jnp.concatenate(parts, axis=axis)


def halves(x):
    width = x.shape[1] // 2
    return x[:, :width] + x[:, width:]


def square_product(a, b):
    ah, al = split(a)
    bh, bl = split(b)
    wide = cat([bh, bl], 1)
    return halves(dot(cat([ah, al], 1), cat([wide, wide], 0)))


def square_product_t(a, b):
    ah, al = split(a)
    bh, bl = split(b)
    wide = cat([bh, bl], 1)
    return halves(dot(cat([ah, al], 0), cat([wide, wide], 0), 0, 0))


def square_product_bt(a, b):
    ah, al = split(a)
    bh, bl = split(b)
    tall = cat([bh, bl], 0)
    return halves(dot(cat([ah, al], 1), cat([tall, tall], 1), 1, 1))


def positions(count):
    shape = (count, count)
    return (lax.broadcasted_iota(jnp.int32, shape, 0), lax.broadcasted_iota(jnp.int32, shape, 1))


def inverses(blocks):
    count = blocks[0].shape[0]
    row, column = positions(count)
    identity = jnp.where(row == column, 1.0, 0.0)
    found = None
    width = 1
    while width < count:
        pairs = (row // (2 * width) == column // (2 * width)) & (row // width != column // width)
        offs = [jnp.where(pairs, block, 0.0) for block in blocks]
        if found is None:
            found = [identity - off for off in offs]
        else:
            firsts = [square_product(inverse, off) for inverse, off in zip(found, offs)]
            found = [
                inverse - square_product(first, inverse) for first, inverse in zip(firsts, found)
            ]
        width *= 2
    return found


def unit_scales(raw, factor):
    data = raw.astype(f32)
    total = jnp.sum(data * data, axis=1, keepdims=True) + eps_norm
    return lax.rsqrt(total) * factor, total


def as_row(column):
    return jnp.transpose(jnp.broadcast_to(column, (column.shape[0], SUB)))[0:1, :]


def chunk_matrices(kr, qr):
    rk, sk = unit_scales(kr, 1.0)
    rq, sq = unit_scales(qr, kr.shape[1] ** (-0.5))
    rk_row = as_row(rk)
    both = dot(cat([kr, qr], 0), kr, 1, 1) * rk_row
    count = kr.shape[0]
    return rk, sk, rq, sq, rk_row, both[:count] * rk, both[count:] * rq


def decay_matrix(g_col, g_row, lower):
    return jnp.exp(jnp.where(lower, g_col - g_row, -1e30))


def before_kernel(
    place_ref, q_ref, k_ref, v_ref, d_ref, rows_ref, cols_ref,
    th_ref, tl_ref, y_ref, z_ref, m_ref, b_ref, p_ref, first_ref,
):
    key_count, count, _ = k_ref.shape
    value_count = v_ref.shape[0]
    share = value_count // key_count
    row, column = positions(count)
    lower = row >= column
    strict = row > column
    rows = rows_ref[...]
    cols = cols_ref[...]
    scales, mixings, systems = [], [], []
    for i in range(key_count):
        kr, qr = k_ref[i], q_ref[i]
        rk, sk, rq, sq, rk_row, key_key, query_key = chunk_matrices(kr, qr)
        for r in range(share):
            h = i * share + r
            g_col, beta = cols[:, h : h + 1], cols[:, value_count + h : value_count + h + 1]
            decay = decay_matrix(g_col, rows[h : h + 1, :], lower)
            systems.append(jnp.where(strict, beta * decay * key_key, 0.0))
            mixings.append(decay * query_key)
            scales.append((rk, rq, beta, g_col))
    pieces = count // SUB
    diagonal = []
    for a in systems:
        for n in range(pieces):
            diagonal.append(a[n * SUB : (n + 1) * SUB, n * SUB : (n + 1) * SUB])
    diagonal = inverses(diagonal)
    identity = jnp.where(positions(SUB)[0] == positions(SUB)[1], 1.0, 0.0)
    for h in range(value_count):
        a = systems[h]
        blocks = [[None] * pieces for _ in range(pieces)]
        for n in range(pieces):
            blocks[n][n] = diagonal[h * pieces + n]
            for m in range(n):
                total = None
                for l in range(m, n):
                    term = square_product(
                        a[n * SUB : (n + 1) * SUB, l * SUB : (l + 1) * SUB], blocks[l][m]
                    )
                    total = term if total is None else total + term
                blocks[n][m] = -square_product(blocks[n][n], total)
            for m in range(n + 1, pieces):
                blocks[n][m] = jnp.zeros((SUB, SUB), f32)
        inverse = cat([cat(line, 1) for line in blocks], 0)
        rk, rq, beta, g_col = scales[h]
        kr, qr, v, d = k_ref[h // share], q_ref[h // share], v_ref[h], d_ref[h]
        width = kr.shape[1]
        last = g_col[count - 1 : count, :]
        growth = jnp.exp(g_col)
        to_end = jnp.exp(last - g_col) * rk
        ph, pl_ = split(mixings[h])
        pulled = dot(ph, d, 0, 0) + dot(pl_, d, 0, 0)
        th, tl = split(inverse)
        keys_h, keys_l = split(to_end * kr.astype(f32))
        pull_h, pull_l = split(pulled)
        high = dot(th, cat([keys_h, pull_h, keys_l, pull_l], 1), 0, 0)
        yz = high[:, : 2 * width] + high[:, 2 * width :]
        yz = yz + dot(tl, cat([keys_h, pull_h], 1), 0, 0)
        y, z = yz[:, :width], yz[:, width:]
        th_ref[h] = th
        tl_ref[h] = tl
        y_ref[h] = y
        z_ref[h] = z
        yb = y * beta
        bh, bl = split(yb)
        base = dot(bh, v, 0, 0) + dot(bl, v, 0, 0)
        mh, ml = split(yb * (growth * rk))
        m_ref[h] = identity * jnp.exp(last) - (dot(mh, kr, 0, 0) + dot(ml, kr, 0, 0))
        outs_h, outs_l = split((growth * rq) * d.astype(f32))
        ins_h, ins_l = split((beta * growth * rk) * z)
        push = halves(
            dot(qr, cat([outs_h, outs_l], 1), 0, 0) - dot(kr, cat([ins_h, ins_l], 1), 0, 0)
        )
        b_ref[h] = base
        p_ref[h] = push
        first_ref[h] = jnp.where(place_ref[0] == 0, base, push)


def relay_kernel(hop, count, place_ref, m_ref, b_ref, p_ref, got_ref, out_ref):
    place = place_ref[0]

    @pl.when(place == hop)
    def _():
        for h in range(m_ref.shape[0]):
            out_ref[h] = square_product(m_ref[h], got_ref[h]) + b_ref[h]

    @pl.when(place == count - 1 - hop)
    def _():
        for h in range(m_ref.shape[0]):
            out_ref[h] = square_product_t(m_ref[h], got_ref[h]) + p_ref[h]


def chosen(place, arrivals, h, first, step):
    total = jnp.zeros(arrivals[0].shape[1:], f32)
    for hop, arrival in enumerate(arrivals):
        total = jnp.where(first + step * place == hop, arrival[h], total)
    return total


def values_kernel(*refs):
    place_ref, q_ref, k_ref, v_ref, d_ref, rows_ref, cols_ref, th_ref, tl_ref, y_ref, z_ref = refs[:11]
    arrivals = refs[11:-7]
    o_ref, dv_ref, n_ref, r_ref, s_ref, e_ref, small_ref = refs[-7:]
    key_count, count, width = k_ref.shape
    value_count = v_ref.shape[0]
    share = value_count // key_count
    row, column = positions(count)
    lower = row >= column
    rows = rows_ref[...]
    cols = cols_ref[...]
    place = place_ref[0]
    gates, logits = [], []
    for i in range(key_count):
        kr, qr = k_ref[i], q_ref[i]
        rk, _ = unit_scales(kr, 1.0)
        rq, _ = unit_scales(qr, width ** (-0.5))
        query_key = dot(qr, kr, 1, 1) * as_row(rk) * rq
        both = cat([qr, kr], 0)
        for r in range(share):
            h = i * share + r
            g_col, beta = cols[:, h : h + 1], cols[:, value_count + h : value_count + h + 1]
            decay = decay_matrix(g_col, rows[h : h + 1, :], lower)
            growth = jnp.exp(g_col)
            v, d = v_ref[h], d_ref[h]
            vf, df = v.astype(f32), d.astype(f32)
            s = chosen(place, arrivals, h, -1, 1)
            e = chosen(place, arrivals, h, len(arrivals) - 1, -1)
            s_ref[h] = s
            e_ref[h] = e
            sh, sl = split(s)
            carried = halves(dot(both, cat([sh, sl], 1)))
            residual = beta * (vf - (growth * rk) * carried[count:])
            rh, rl = split(residual)
            th, tl = th_ref[h], tl_ref[h]
            new = halves(dot(th, cat([rh, rl], 1))) + dot(tl, rh)
            n_ref[h] = new
            nh, nl = split(new)
            ph, pl_ = split(decay * query_key)
            out = (growth * rq) * carried[:count] + halves(dot(ph, cat([nh, nl], 1))) + dot(pl_, nh)
            o_ref[h] = out.astype(bf16)
            d_res = z_ref[h] + square_product(y_ref[h], e)
            r_ref[h] = d_res
            dv = beta * d_res
            dv_ref[h] = dv.astype(bf16)
            logits.append((1.0 - beta) * jnp.sum(d_res * new, axis=1, keepdims=True))
            gates.append(jnp.sum(df * out - dv * vf, axis=1, keepdims=True))
    after = jnp.where(row <= column, 1.0, 0.0).astype(bf16)
    gh, gl = split(cat(gates, 1))
    small_ref[...] = cat([halves(dot(after, cat([gh, gl], 1)))] + logits, 1)


def keys_kernel(
    q_ref, k_ref, d_ref, rows_ref, cols_ref, n_ref, r_ref, s_ref, e_ref, small_ref,
    dq_ref, dk_ref, gate_ref,
):
    key_count, count, width = k_ref.shape
    value_count = d_ref.shape[0]
    share = value_count // key_count
    row, column = positions(count)
    lower = row >= column
    strict = row > column
    rows = rows_ref[...]
    cols = cols_ref[...]
    gates = []
    for i in range(key_count):
        kr, qr = k_ref[i], q_ref[i]
        kf, qf = kr.astype(f32), qr.astype(f32)
        rk, sk = unit_scales(kr, 1.0)
        rq, sq = unit_scales(qr, width ** (-0.5))
        rk_row = as_row(rk)
        mix_grad = pair_grad = dq = dk = None
        for r in range(share):
            h = i * share + r
            g_col, beta = cols[:, h : h + 1], cols[:, value_count + h : value_count + h + 1]
            decay = decay_matrix(g_col, rows[h : h + 1, :], lower)
            growth = jnp.exp(g_col)
            last = g_col[count - 1 : count, :]
            to_end = jnp.exp(last - g_col)
            d = d_ref[h]
            s, e, new, d_res = s_ref[h], e_ref[h], n_ref[h], r_ref[h]
            sh, sl = split(s)
            nh, nl = split(new)
            drh, drl = split(d_res)
            tall = cat([nh, nl], 1)
            d_mix = dot(cat([d, d], 1), tall, 1, 1)
            d_sys = dot(cat([drh, drh], 1), tall, 1, 1) + dot(drl, nh, 1, 1)
            term = decay * d_mix
            mix_grad = term if mix_grad is None else mix_grad + term
            term = jnp.where(strict, beta * decay * d_sys, 0.0)
            pair_grad = term if pair_grad is None else pair_grad + term
            term = growth * dot(cat([d, d], 1), cat([sh, sl], 1), 1, 1)
            dq = term if dq is None else dq + term
            from_end = to_end * square_product_bt(new, e)
            from_in = (growth * beta) * square_product_bt(d_res, s)
            total = jnp.sum(from_end * kf * rk, axis=0, keepdims=True) + jnp.exp(last) * jnp.sum(
                s * e, axis=0, keepdims=True
            )
            gates.append(jnp.sum(total, axis=1, keepdims=True))
            term = from_end - from_in
            dk = term if dk is None else dk + term
        mh, ml = split(mix_grad * rk_row)
        dq = dq + dot(mh, kr) + dot(ml, kr)
        xh, xl = split(mix_grad * rq)
        dk = dk + dot(xh, qr, 0, 0) + dot(xl, qr, 0, 0)
        gh, gl = split(pair_grad * rk_row)
        dk = dk - (dot(gh, kr) + dot(gl, kr))
        gh, gl = split(pair_grad * rk)
        dk = dk - (dot(gh, kr, 0, 0) + dot(gl, kr, 0, 0))
        along = jnp.sum(qf * dq, axis=1, keepdims=True)
        dq_ref[i] = (rq * (dq - qf * (along / sq))).astype(bf16)
        along = jnp.sum(kf * dk, axis=1, keepdims=True)
        dk_ref[i] = (rk * (dk - kf * (along / sk))).astype(bf16)
    gate_ref[...] = small_ref[...][:, :value_count] + cat(gates, 1)


def call(kernel, name, operands, outs, flops):
    return pl.pallas_call(
        kernel,
        name=name,
        in_specs=[
            pl.BlockSpec(memory_space=pltpu.SMEM if x.dtype == jnp.int32 else pltpu.VMEM)
            for x in operands
        ],
        out_specs=[pl.BlockSpec(memory_space=pltpu.VMEM)] * len(outs),
        out_shape=[jax.ShapeDtypeStruct(shape, kind) for shape, kind in outs],
        compiler_params=pltpu.CompilerParams(vmem_limit_bytes=VMEM),
        cost_estimate=pl.CostEstimate(flops=flops, bytes_accessed=1 << 20, transcendentals=0),
    )(*operands)


def strided(kernel, name, tokens, operands, outs, scratch_rows):
    def block(shape, axis):
        sizes = tuple(SUB if n == axis else size for n, size in enumerate(shape))
        return pl.BlockSpec(sizes, lambda step: tuple(step if n == axis else 0 for n in range(len(shape))))

    return pl.pallas_call(
        kernel,
        name=name,
        grid=(tokens // SUB,),
        in_specs=[block(x.shape, axis) for x, axis in operands],
        out_specs=[block(shape, axis) for shape, _, axis in outs],
        out_shape=[jax.ShapeDtypeStruct(shape, kind) for shape, kind, _ in outs],
        scratch_shapes=[pltpu.VMEM((SUB * scratch_rows, SUB), f32), pltpu.VMEM((scratch_rows, 1), f32)],
        compiler_params=pltpu.CompilerParams(vmem_limit_bytes=VMEM),
        cost_estimate=pl.CostEstimate(flops=1 << 24, bytes_accessed=1 << 23, transcendentals=0),
    )(*[x for x, _ in operands])


def turned(parts):
    count = sum(part.shape[1] for part in parts)
    filler = jnp.zeros((parts[0].shape[0], SUB - count), f32)
    return jnp.transpose(cat(parts + [filler], 1))[:count]


def arrange_kernel(nk, nv, *refs):
    q_ref, k_ref, v_ref, d_ref, hidden_ref, weight_ref, bias_ref, rate_ref = refs[:8]
    outs, (wide_ref, total_ref) = refs[8:-2], refs[-2:]
    parts = len(outs) // 6
    for n, ref in enumerate((q_ref, k_ref, v_ref, d_ref)):
        count, heads, width = ref.shape
        group = heads // parts
        wide_ref[0 : count * heads, :] = ref[...].astype(f32).reshape(count * heads, width)
        for h in range(heads):
            outs[n * parts + h // group][h % group] = wide_ref[
                pl.ds(h, count, stride=heads), :
            ].astype(bf16)
    beta = jax.nn.sigmoid(dot(weight_ref[...], hidden_ref[...], 1, 1) + bias_ref[...])

    @pl.when(pl.program_id(0) == 0)
    def _():
        total_ref[...] = jnp.zeros_like(total_ref)

    rates = rate_ref[...]
    heads = rates.shape[0]
    high, low = split(rates)
    rest = (rates - high.astype(f32) - low.astype(f32)).astype(bf16)
    row, column = positions(rates.shape[1])
    before = jnp.where(row <= column, 1.0, 0.0).astype(bf16)
    sums = dot(cat([high, low, rest], 0), before)
    summed = sums[:heads] + sums[heads : 2 * heads] + sums[2 * heads :] + total_ref[0:heads]
    total_ref[0:heads] = summed[:, -1:]
    filler = jnp.zeros((SUB - 2 * heads, rates.shape[1]), f32)
    cols = jnp.transpose(cat([summed, beta, filler], 0))
    for part in range(parts):
        first = part * nv
        outs[4 * parts + part][...] = cat([summed[first : first + nv], beta[first : first + nv]], 0)
        outs[5 * parts + part][...] = cat(
            [cols[:, first : first + nv], cols[:, heads + first : heads + first + nv]], 1
        )


def weight_kernel(nv, *refs):
    smalls, (hidden_ref, part_ref, logit_ref) = refs[:-3], refs[-3:]
    rows = [turned([ref[n * SUB : (n + 1) * SUB, nv : 2 * nv] for ref in smalls]) for n in range(smalls[0].shape[0] // SUB)]
    rows = cat(rows, 1)
    logit_ref[...] = rows
    heads = rows.shape[0]
    both = dot(cat(split(rows), 0), hidden_ref[...])
    part_ref[...] = both[:heads] + both[heads:]


def finish_kernel(*refs):
    logit_ref, other_ref, weight_ref, other_weight_ref = refs[:4]
    ins, outs, (wide_ref, _) = refs[4:-8], refs[-8:-2], refs[-2:]
    parts = len(ins) // 5
    for n in range(4):
        out_ref = outs[n]
        count, heads, width = out_ref.shape
        group = heads // parts
        for h in range(heads):
            wide_ref[pl.ds(h, count, stride=heads), :] = ins[n * parts + h // group][h % group].astype(f32)
        out_ref[...] = wide_ref[0 : count * heads, :].reshape(count, heads, width).astype(bf16)
    outs[4][...] = turned([ref[...] for ref in ins[4 * parts :]])
    high, low = split(cat([logit_ref[...], other_ref[...]], 0))
    weight = cat([weight_ref[...], other_weight_ref[...]], 0)
    outs[5][...] = dot(cat([high, low], 0), cat([weight, weight], 0), 0, 0).astype(bf16)


def exchanged(value, axis, step):
    pairs = [(i, i ^ step) for i in range(lax.axis_size(axis))]
    return value + lax.ppermute(value, axis, pairs)


def on_device(queries, keys_in, values, hidden_in, beta_weight, beta_bias, log_gate, out_grad):
    _, tokens, model_width = hidden_in.shape
    key_heads, key_dim = queries.shape[2:]
    value_heads, value_dim = values.shape[2:]
    nk = KEY_GROUP
    nv = nk * value_heads // key_heads
    parts = key_heads // nk
    count = lax.axis_size("seq")
    place = lax.axis_index("seq").astype(jnp.int32).reshape(1)
    hidden = hidden_in.reshape(tokens, model_width)
    weight = beta_weight.T

    narrow = (nk, tokens, key_dim)
    chunk = (nv, tokens, value_dim)
    state = (nv, key_dim, value_dim)
    square = (nv, tokens, tokens)
    work = nv * 2 * tokens**3
    arranged = strided(
        functools.partial(arrange_kernel, nk, nv), "arrange", tokens,
        (
            (queries[0], 0), (keys_in[0], 0), (values[0], 0), (out_grad[0], 0), (hidden, 0),
            (weight, None), (beta_bias.reshape(value_heads, 1), None), (log_gate[0].T, 1),
        ),
        [(narrow, bf16, 1)] * (2 * parts) + [(chunk, bf16, 1)] * (2 * parts)
        + [((2 * nv, tokens), f32, 1)] * parts + [((tokens, 2 * nv), f32, 0)] * parts,
        value_heads,
    )
    q, k, v, d, rows, cols = [arranged[n * parts : (n + 1) * parts] for n in range(6)]
    befores = []
    for part in range(parts):
        befores.append(
            call(
                before_kernel, "before",
                (place, q[part], k[part], v[part], d[part], rows[part], cols[part]),
                ((square, bf16), (square, bf16), (chunk, f32), (chunk, f32)) + ((state, f32),) * 4,
                60 * work,
            )
        )
    sends = [b[7] for b in befores]
    arrivals = [[] for _ in range(parts)]
    for hop in range(count - 1):
        for part in range(parts):
            if hop:
                (sends[part],) = call(
                    functools.partial(relay_kernel, hop, count), "relay",
                    (place, *befores[part][4:7], arrivals[part][-1]), ((state, f32),), work // 4,
                )
            route = [(hop, hop + 1), (count - 1 - hop, count - 2 - hop)]
            arrivals[part].append(lax.ppermute(sends[part], "seq", route))
    firsts = []
    for part in range(parts):
        firsts.append(
            call(
                values_kernel, "values",
                (
                    place, q[part], k[part], v[part], d[part], rows[part], cols[part],
                    *befores[part][:4], *arrivals[part],
                ),
                (
                    (chunk, bf16), (chunk, bf16), (chunk, f32), (chunk, f32), (state, f32), (state, f32),
                    ((tokens, 2 * nv), f32),
                ),
                20 * work,
            )
        )
    grad_weight, grad_logits = call(
        functools.partial(weight_kernel, nv), "weight", (*[a[6] for a in firsts], hidden),
        (((value_heads, model_width), f32), ((value_heads, tokens), f32)), work // 4,
    )
    here = lax.axis_index("head")
    half = model_width // 2
    swap = [(0, 1), (1, 0)]
    weight_here = lax.dynamic_slice_in_dim(weight, here * half, half, 1)
    weight_there = lax.dynamic_slice_in_dim(weight, (1 - here) * half, half, 1)
    other_weight = lax.ppermute(weight_there, "head", swap)
    other_logits = lax.ppermute(grad_logits, "head", swap)
    seconds = []
    rounds = [
        (axis, 1 << n) for axis in ("dp", "seq") for n in range((lax.axis_size(axis) - 1).bit_length())
    ]
    for part in range(parts):
        _, _, n, r, s, e, small = firsts[part]
        if part:
            small, grad_weight = lax.optimization_barrier((small, grad_weight))
        for axis, step in rounds[part :] if part == parts - 1 else rounds[part : part + 1]:
            grad_weight = exchanged(grad_weight, axis, step)
        seconds.append(
            call(
                keys_kernel, "keys", (q[part], k[part], d[part], rows[part], cols[part], n, r, s, e, small),
                ((narrow, bf16), (narrow, bf16), ((tokens, nv), f32)), 20 * work,
            )
        )
    attended, grad_values, grad_query, grad_key, grad_gate, grad_hidden = strided(
        finish_kernel, "finish", tokens,
        [(grad_logits, 1), (other_logits, 1), (weight_here, None), (other_weight, None)]
        + [(a[0], 1) for a in firsts] + [(a[1], 1) for a in firsts]
        + [(a[0], 1) for a in seconds] + [(a[1], 1) for a in seconds] + [(a[2], 0) for a in seconds],
        [
            ((tokens, value_heads, value_dim), bf16, 0), ((tokens, value_heads, value_dim), bf16, 0),
            ((tokens, key_heads, key_dim), bf16, 0), ((tokens, key_heads, key_dim), bf16, 0),
            ((value_heads, tokens), f32, 1), ((tokens, half), bf16, 0),
        ],
        value_heads,
    )
    return (
        attended[None], grad_query[None], grad_key[None], grad_values[None], grad_gate.T[None],
        grad_hidden[None], grad_weight.T,
    )


def solution(mesh):
    heads = P("dp", "seq", "head", None)
    return jax.shard_map(
        on_device,
        mesh=mesh,
        in_specs=(
            heads, heads, heads, P("dp", "seq", None), P(None, "head"), P("head"),
            P("dp", "seq", "head"), heads,
        ),
        out_specs=(
            heads, heads, heads, heads, P("dp", "seq", "head"), P("dp", "seq", "head"), P(None, "head"),
        ),
        check_vma=False,
    )
```

```python
import functools

import jax
import jax.numpy as jnp
from jax import lax
from jax.experimental import pallas as pl
from jax.experimental.pallas import tpu as pltpu
from jax.sharding import PartitionSpec as P

SUB = 128
KEY_GROUP = 2
VMEM = 24 * 1024 * 1024
WHOLE = 56 * 1024 * 1024

eps_norm = 1e-06
f32 = jnp.float32
bf16 = jnp.bfloat16


def split(x):
    high = x.astype(bf16)
    return high, (x - high.astype(f32)).astype(bf16)


def dot(a, b, ca=1, cb=0):
    return lax.dot_general(a, b, (((ca,), (cb,)), ((), ())), preferred_element_type=f32)


def cat(parts, axis):
    return jnp.concatenate(parts, axis=axis)


def halves(x):
    width = x.shape[1] // 2
    return x[:, :width] + x[:, width:]


def square_product(a, b):
    ah, al = split(a)
    bh, bl = split(b)
    wide = cat([bh, bl], 1)
    return halves(dot(cat([ah, al], 1), cat([wide, wide], 0)))


def square_product_t(a, b):
    ah, al = split(a)
    bh, bl = split(b)
    wide = cat([bh, bl], 1)
    return halves(dot(cat([ah, al], 0), cat([wide, wide], 0), 0, 0))


def square_product_bt(a, b):
    ah, al = split(a)
    bh, bl = split(b)
    tall = cat([bh, bl], 0)
    return halves(dot(cat([ah, al], 1), cat([tall, tall], 1), 1, 1))


def positions(count):
    shape = (count, count)
    return (lax.broadcasted_iota(jnp.int32, shape, 0), lax.broadcasted_iota(jnp.int32, shape, 1))


def inverses(blocks):
    count = blocks[0].shape[0]
    row, column = positions(count)
    identity = jnp.where(row == column, 1.0, 0.0)
    found = None
    width = 1
    while width < count:
        pairs = (row // (2 * width) == column // (2 * width)) & (row // width != column // width)
        offs = [jnp.where(pairs, block, 0.0) for block in blocks]
        if found is None:
            found = [identity - off for off in offs]
        else:
            firsts = [square_product(inverse, off) for inverse, off in zip(found, offs)]
            found = [
                inverse - square_product(first, inverse) for first, inverse in zip(firsts, found)
            ]
        width *= 2
    return found


def unit_scales(raw, factor):
    data = raw.astype(f32)
    total = jnp.sum(data * data, axis=1, keepdims=True) + eps_norm
    return lax.rsqrt(total) * factor, total


def as_row(column):
    return jnp.transpose(jnp.broadcast_to(column, (column.shape[0], SUB)))[0:1, :]


def chunk_matrices(kr, qr):
    rk, sk = unit_scales(kr, 1.0)
    rq, sq = unit_scales(qr, kr.shape[1] ** (-0.5))
    rk_row = as_row(rk)
    both = dot(cat([kr, qr], 0), kr, 1, 1) * rk_row
    count = kr.shape[0]
    return rk, sk, rq, sq, rk_row, both[:count] * rk, both[count:] * rq


def decay_matrix(g_col, g_row, lower):
    return jnp.exp(jnp.where(lower, g_col - g_row, -1e30))


def before_kernel(
    place_ref, q_ref, k_ref, v_ref, d_ref, rows_ref, cols_ref,
    th_ref, tl_ref, y_ref, z_ref, m_ref, b_ref, p_ref, first_ref,
    th_held, tl_held, y_held, z_held, sems,
):
    key_count, count, _ = k_ref.shape
    value_count = v_ref.shape[0]
    share = value_count // key_count
    row, column = positions(count)
    lower = row >= column
    strict = row > column
    rows = rows_ref[...]
    cols = cols_ref[...]
    scales, mixings, systems = [], [], []
    for i in range(key_count):
        kr, qr = k_ref[i], q_ref[i]
        rk, sk, rq, sq, rk_row, key_key, query_key = chunk_matrices(kr, qr)
        for r in range(share):
            h = i * share + r
            g_col, beta = cols[:, h : h + 1], cols[:, value_count + h : value_count + h + 1]
            decay = decay_matrix(g_col, rows[h : h + 1, :], lower)
            systems.append(jnp.where(strict, beta * decay * key_key, 0.0))
            mixings.append(decay * query_key)
            scales.append((rk, rq, beta, g_col))
    pieces = count // SUB
    diagonal = []
    for a in systems:
        for n in range(pieces):
            diagonal.append(a[n * SUB : (n + 1) * SUB, n * SUB : (n + 1) * SUB])
    diagonal = inverses(diagonal)
    identity = jnp.where(positions(SUB)[0] == positions(SUB)[1], 1.0, 0.0)
    copies = []

    def leave(n, held, ref):
        copies.append(pltpu.make_async_copy(held, ref, sems.at[n]))
        copies[-1].start()

    for h in range(value_count):
        a = systems[h]
        blocks = [[None] * pieces for _ in range(pieces)]
        for n in range(pieces):
            blocks[n][n] = diagonal[h * pieces + n]
            for m in range(n):
                total = None
                for l in range(m, n):
                    term = square_product(
                        a[n * SUB : (n + 1) * SUB, l * SUB : (l + 1) * SUB], blocks[l][m]
                    )
                    total = term if total is None else total + term
                blocks[n][m] = -square_product(blocks[n][n], total)
            for m in range(n + 1, pieces):
                blocks[n][m] = jnp.zeros((SUB, SUB), f32)
        th_held[h], tl_held[h] = split(cat([cat(line, 1) for line in blocks], 0))
    leave(0, th_held, th_ref)
    leave(1, tl_held, tl_ref)
    for h in range(value_count):
        rk, rq, beta, g_col = scales[h]
        kr, qr, v, d = k_ref[h // share], q_ref[h // share], v_ref[h], d_ref[h]
        width = kr.shape[1]
        last = g_col[count - 1 : count, :]
        growth = jnp.exp(g_col)
        to_end = jnp.exp(last - g_col) * rk
        ph, pl_ = split(mixings[h])
        pulled = dot(ph, d, 0, 0) + dot(pl_, d, 0, 0)
        th, tl = th_held[h], tl_held[h]
        keys_h, keys_l = split(to_end * kr.astype(f32))
        pull_h, pull_l = split(pulled)
        high = dot(th, cat([keys_h, pull_h, keys_l, pull_l], 1), 0, 0)
        yz = high[:, : 2 * width] + high[:, 2 * width :]
        yz = yz + dot(tl, cat([keys_h, pull_h], 1), 0, 0)
        y, z = yz[:, :width], yz[:, width:]
        y_held[h] = y
        z_held[h] = z
        yb = y * beta
        bh, bl = split(yb)
        base = dot(bh, v, 0, 0) + dot(bl, v, 0, 0)
        mh, ml = split(yb * (growth * rk))
        m_ref[h] = identity * jnp.exp(last) - (dot(mh, kr, 0, 0) + dot(ml, kr, 0, 0))
        outs_h, outs_l = split((growth * rq) * d.astype(f32))
        ins_h, ins_l = split((beta * growth * rk) * z)
        push = halves(
            dot(qr, cat([outs_h, outs_l], 1), 0, 0) - dot(kr, cat([ins_h, ins_l], 1), 0, 0)
        )
        b_ref[h] = base
        p_ref[h] = push
        first_ref[h] = jnp.where(place_ref[0] == 0, base, push)
    leave(2, y_held, y_ref)
    leave(3, z_held, z_ref)
    for copy in copies:
        copy.wait()


def relay_kernel(hops, count, place_ref, *refs):
    place, out_ref = place_ref[0], refs[-1]
    at = 0
    for hop in hops:
        if hop == 0:
            first_ref = refs[at]
            at += 1

            @pl.when((place == 0) | (place == count - 1))
            def _():
                out_ref[...] = first_ref[...]

            continue
        m_ref, b_ref, p_ref, got_ref = refs[at : at + 4]
        at += 4

        @pl.when(place == hop)
        def _():
            for h in range(m_ref.shape[0]):
                out_ref[h] = square_product(m_ref[h], got_ref[h]) + b_ref[h]

        @pl.when(place == count - 1 - hop)
        def _():
            for h in range(m_ref.shape[0]):
                out_ref[h] = square_product_t(m_ref[h], got_ref[h]) + p_ref[h]


def chosen(place, arrivals, h, first, step):
    total = jnp.zeros(arrivals[0].shape[1:], f32)
    for hop, arrival in enumerate(arrivals):
        total = jnp.where(first + step * place == hop, arrival[h], total)
    return total


def values_kernel(*refs):
    place_ref, q_ref, k_ref, v_ref, d_ref, rows_ref, cols_ref, th_ref, tl_ref, y_ref, z_ref = refs[:11]
    arrivals = refs[11:-7]
    o_ref, dv_ref, n_ref, r_ref, s_ref, e_ref, small_ref = refs[-7:]
    key_count, count, width = k_ref.shape
    value_count = v_ref.shape[0]
    share = value_count // key_count
    row, column = positions(count)
    lower = row >= column
    rows = rows_ref[...]
    cols = cols_ref[...]
    place = place_ref[0]
    gates, logits = [], []
    for i in range(key_count):
        kr, qr = k_ref[i], q_ref[i]
        rk, _ = unit_scales(kr, 1.0)
        rq, _ = unit_scales(qr, width ** (-0.5))
        query_key = dot(qr, kr, 1, 1) * as_row(rk) * rq
        both = cat([qr, kr], 0)
        for r in range(share):
            h = i * share + r
            g_col, beta = cols[:, h : h + 1], cols[:, value_count + h : value_count + h + 1]
            decay = decay_matrix(g_col, rows[h : h + 1, :], lower)
            growth = jnp.exp(g_col)
            v, d = v_ref[h], d_ref[h]
            vf, df = v.astype(f32), d.astype(f32)
            s = chosen(place, arrivals, h, -1, 1)
            e = chosen(place, arrivals, h, len(arrivals) - 1, -1)
            s_ref[h] = s
            e_ref[h] = e
            sh, sl = split(s)
            carried = halves(dot(both, cat([sh, sl], 1)))
            residual = beta * (vf - (growth * rk) * carried[count:])
            rh, rl = split(residual)
            th, tl = th_ref[h], tl_ref[h]
            new = halves(dot(th, cat([rh, rl], 1))) + dot(tl, rh)
            n_ref[h] = new
            nh, nl = split(new)
            ph, pl_ = split(decay * query_key)
            out = (growth * rq) * carried[:count] + halves(dot(ph, cat([nh, nl], 1))) + dot(pl_, nh)
            o_ref[h] = out.astype(bf16)
            d_res = z_ref[h] + square_product(y_ref[h], e)
            r_ref[h] = d_res
            dv = beta * d_res
            dv_ref[h] = dv.astype(bf16)
            logits.append((1.0 - beta) * jnp.sum(d_res * new, axis=1, keepdims=True))
            gates.append(jnp.sum(df * out - dv * vf, axis=1, keepdims=True))
    after = jnp.where(row <= column, 1.0, 0.0).astype(bf16)
    gh, gl = split(cat(gates, 1))
    small_ref[...] = cat([halves(dot(after, cat([gh, gl], 1)))] + logits, 1)


def keys_kernel(
    q_ref, k_ref, d_ref, rows_ref, cols_ref, n_ref, r_ref, s_ref, e_ref, small_ref,
    dq_ref, dk_ref, gate_ref,
):
    key_count, count, width = k_ref.shape
    value_count = d_ref.shape[0]
    share = value_count // key_count
    row, column = positions(count)
    lower = row >= column
    strict = row > column
    rows = rows_ref[...]
    cols = cols_ref[...]
    gates = []
    for i in range(key_count):
        kr, qr = k_ref[i], q_ref[i]
        kf, qf = kr.astype(f32), qr.astype(f32)
        rk, sk = unit_scales(kr, 1.0)
        rq, sq = unit_scales(qr, width ** (-0.5))
        rk_row = as_row(rk)
        mix_grad = pair_grad = dq = dk = None
        for r in range(share):
            h = i * share + r
            g_col, beta = cols[:, h : h + 1], cols[:, value_count + h : value_count + h + 1]
            decay = decay_matrix(g_col, rows[h : h + 1, :], lower)
            growth = jnp.exp(g_col)
            last = g_col[count - 1 : count, :]
            to_end = jnp.exp(last - g_col)
            d = d_ref[h]
            s, e, new, d_res = s_ref[h], e_ref[h], n_ref[h], r_ref[h]
            sh, sl = split(s)
            nh, nl = split(new)
            drh, drl = split(d_res)
            tall = cat([nh, nl], 1)
            d_mix = dot(cat([d, d], 1), tall, 1, 1)
            d_sys = dot(cat([drh, drh], 1), tall, 1, 1) + dot(drl, nh, 1, 1)
            term = decay * d_mix
            mix_grad = term if mix_grad is None else mix_grad + term
            term = jnp.where(strict, beta * decay * d_sys, 0.0)
            pair_grad = term if pair_grad is None else pair_grad + term
            term = growth * dot(cat([d, d], 1), cat([sh, sl], 1), 1, 1)
            dq = term if dq is None else dq + term
            from_end = to_end * square_product_bt(new, e)
            from_in = (growth * beta) * square_product_bt(d_res, s)
            total = jnp.sum(from_end * kf * rk, axis=0, keepdims=True) + jnp.exp(last) * jnp.sum(
                s * e, axis=0, keepdims=True
            )
            gates.append(jnp.sum(total, axis=1, keepdims=True))
            term = from_end - from_in
            dk = term if dk is None else dk + term
        mh, ml = split(mix_grad * rk_row)
        dq = dq + dot(mh, kr) + dot(ml, kr)
        xh, xl = split(mix_grad * rq)
        dk = dk + dot(xh, qr, 0, 0) + dot(xl, qr, 0, 0)
        gh, gl = split(pair_grad * rk_row)
        dk = dk - (dot(gh, kr) + dot(gl, kr))
        gh, gl = split(pair_grad * rk)
        dk = dk - (dot(gh, kr, 0, 0) + dot(gl, kr, 0, 0))
        along = jnp.sum(qf * dq, axis=1, keepdims=True)
        dq_ref[i] = (rq * (dq - qf * (along / sq))).astype(bf16)
        along = jnp.sum(kf * dk, axis=1, keepdims=True)
        dk_ref[i] = (rk * (dk - kf * (along / sk))).astype(bf16)
    gate_ref[...] = small_ref[...][:, :value_count] + cat(gates, 1)


def call(kernel, name, operands, outs, flops, far_ins=(), far_outs=(), scratch=(), limit=VMEM):
    def spec(n, kind, far):
        space = pltpu.SMEM if kind == jnp.int32 else pltpu.HBM if n in far else pltpu.VMEM
        return pl.BlockSpec(memory_space=space)

    return pl.pallas_call(
        kernel,
        name=name,
        in_specs=[spec(n, x.dtype, far_ins) for n, x in enumerate(operands)],
        out_specs=[spec(n, kind, far_outs) for n, (_, kind) in enumerate(outs)],
        out_shape=[jax.ShapeDtypeStruct(shape, kind) for shape, kind in outs],
        scratch_shapes=list(scratch),
        compiler_params=pltpu.CompilerParams(vmem_limit_bytes=limit),
        cost_estimate=pl.CostEstimate(flops=flops, bytes_accessed=1 << 20, transcendentals=0),
    )(*operands)


def turned(parts):
    count = sum(part.shape[1] for part in parts)
    filler = jnp.zeros((parts[0].shape[0], SUB - count), f32)
    return jnp.transpose(cat(parts + [filler], 1))[:count]


def arrange_kernel(nk, nv, *refs):
    sems, wide_ref = refs[-1], refs[-2]
    held = refs[-10:-2]
    outs = refs[8:-10]
    copies = [
        pltpu.make_async_copy(ref, into, sems.at[n]) for n, (ref, into) in enumerate(zip(refs[:8], held))
    ]
    for copy in copies:
        copy.start()
    parts = len(outs) // 6
    copies[0].wait()
    rates = held[0][...]
    heads = rates.shape[0]
    high, low = split(rates)
    rest = (rates - high.astype(f32) - low.astype(f32)).astype(bf16)
    row, column = positions(rates.shape[1])
    before = jnp.where(row <= column, 1.0, 0.0).astype(bf16)
    sums = dot(cat([high, low, rest], 0), before)
    summed = sums[:heads] + sums[heads : 2 * heads] + sums[2 * heads :]
    for n in range(4):
        copies[3 + n].wait()
        ref = held[3 + n]
        count, each, width = ref.shape
        group = each // parts
        for part in range(parts):
            turn = jnp.swapaxes(ref[:, part * group : (part + 1) * group, :].astype(f32), 0, 1)
            outs[n * parts + part][...] = turn.astype(bf16)
    for n in (1, 2, 7):
        copies[n].wait()
    row, column = positions(heads)
    bias = jnp.sum(jnp.where(row == column, held[1][...], 0.0), axis=1, keepdims=True)
    beta = jax.nn.sigmoid(dot(held[2][...], held[7][...], 1, 1) + bias)
    filler = jnp.zeros((SUB - 2 * heads, rates.shape[1]), f32)
    cols = jnp.transpose(cat([summed, beta, filler], 0))
    for part in range(parts):
        first = part * nv
        outs[4 * parts + part][...] = cat([summed[first : first + nv], beta[first : first + nv]], 0)
        outs[5 * parts + part][...] = cat(
            [cols[:, first : first + nv], cols[:, heads + first : heads + first + nv]], 1
        )


def weight_kernel(nv, *refs):
    smalls, (hidden_ref, part_ref, logit_ref) = refs[:-3], refs[-3:]
    rows = [turned([ref[n * SUB : (n + 1) * SUB, nv : 2 * nv] for ref in smalls]) for n in range(smalls[0].shape[0] // SUB)]
    rows = cat(rows, 1)
    logit_ref[...] = rows
    heads = rows.shape[0]
    both = dot(cat(split(rows), 0), hidden_ref[...])
    part_ref[...] = both[:heads] + both[heads:]


def finish_kernel(parts, *refs):
    logit_ref, other_ref, weight_ref, other_weight_ref = refs[:4]
    ins, outs, gate_ref = refs[4 : 4 + 5 * parts], refs[4 + 5 * parts : -8], refs[-8]
    held, wide_ref, sems = refs[-7:-2], refs[-2], refs[-1]
    copies = [
        pltpu.make_async_copy(held[n], outs[n], sems.at[n]) for n in range(5)
    ]
    for n in range(4):
        count, heads, width = held[n].shape
        group = heads // parts
        whole = cat([ref[...].astype(f32) for ref in ins[n * parts : (n + 1) * parts]], 0)
        held[n][...] = jnp.swapaxes(whole, 0, 1).astype(bf16)
        copies[n].start()
        if n == 1:
            high, low = split(cat([logit_ref[...], other_ref[...]], 0))
            weight = cat([weight_ref[...], other_weight_ref[...]], 0)
            held[4][...] = dot(cat([high, low], 0), cat([weight, weight], 0), 0, 0).astype(bf16)
            copies[4].start()
    gates = ins[4 * parts :]
    for n in range(gate_ref.shape[1] // SUB):
        here = slice(n * SUB, (n + 1) * SUB)
        gate_ref[:, here] = turned([ref[here, :] for ref in gates])
    for copy in copies:
        copy.wait()


def exchanged(value, axis, step):
    pairs = [(i, i ^ step) for i in range(lax.axis_size(axis))]
    return value + lax.ppermute(value, axis, pairs)


def on_device(queries, keys_in, values, hidden_in, beta_weight, beta_bias, log_gate, out_grad):
    _, tokens, model_width = hidden_in.shape
    key_heads, key_dim = queries.shape[2:]
    value_heads, value_dim = values.shape[2:]
    nk = KEY_GROUP
    nv = nk * value_heads // key_heads
    parts = key_heads // nk
    count = lax.axis_size("seq")
    place = lax.axis_index("seq").astype(jnp.int32).reshape(1)
    hidden = hidden_in.reshape(tokens, model_width)
    weight = beta_weight.T

    narrow = (nk, tokens, key_dim)
    chunk = (nv, tokens, value_dim)
    state = (nv, key_dim, value_dim)
    square = (nv, tokens, tokens)
    work = nv * 2 * tokens**3
    inputs = (
        log_gate[0].T, beta_bias.reshape(1, value_heads), weight,
        queries[0], keys_in[0], values[0], out_grad[0], hidden,
    )
    arranged = call(
        functools.partial(arrange_kernel, nk, nv), "arrange", inputs,
        [(narrow, bf16)] * (2 * parts) + [(chunk, bf16)] * (2 * parts)
        + [((2 * nv, tokens), f32)] * parts + [((tokens, 2 * nv), f32)] * parts,
        work, far_ins=range(len(inputs)), limit=WHOLE,
        scratch=[pltpu.VMEM(x.shape, x.dtype) for x in inputs]
        + [pltpu.VMEM((tokens * value_heads, key_dim), f32), pltpu.SemaphoreType.DMA((len(inputs),))],
    )
    q, k, v, d, rows, cols = [list(arranged[n * parts : (n + 1) * parts]) for n in range(6)]

    def before(part):
        return call(
            before_kernel, "before",
            (place, q[part], k[part], v[part], d[part], rows[part], cols[part]),
            ((square, bf16), (square, bf16), (chunk, f32), (chunk, f32)) + ((state, f32),) * 4,
            60 * work, far_outs=range(4), limit=WHOLE,
            scratch=[pltpu.VMEM(square, bf16)] * 2 + [pltpu.VMEM(chunk, f32)] * 2
            + [pltpu.SemaphoreType.DMA((4,))],
        )

    def relay(stage, hops):
        operands = [place]
        for hop in hops:
            made = befores[stage - hop]
            operands += made[4:7] + [arrivals[stage - hop][-1]] if hop else [made[7]]
        if hops == [0]:
            return operands[1]
        (send,) = call(
            functools.partial(relay_kernel, hops, count), "relay", operands, ((state, f32),), work // 4,
        )
        return send

    def new_values(part):
        return call(
            values_kernel, "values",
            (
                place, q[part], k[part], v[part], d[part], rows[part], cols[part],
                *befores[part][:4], *arrivals[part],
            ),
            (
                (chunk, bf16), (chunk, bf16), (chunk, f32), (chunk, f32), (state, f32), (state, f32),
                ((tokens, 2 * nv), f32),
            ),
            20 * work,
        )

    befores, firsts = [], []
    arrivals = [[] for _ in range(parts)]
    shift = max(parts, count)
    for stage in range(shift + parts):
        if stage < parts:
            befores.append([*before(stage)])
        elif stage >= shift:
            firsts.append(new_values(stage - shift))
        due = [hop for hop in range(count - 1) if 0 <= stage - hop < parts]
        due = [hops for hops in ([h for h in due if h % 2], [h for h in due if not h % 2]) if hops]
        sends = [relay(stage, hops) for hops in due]
        following = stage + 1 if stage + 1 < parts else stage + 1 - shift
        if sends and 0 <= following < parts:
            tied = lax.optimization_barrier((rows[following], *sends))
            rows[following] = tied[0]
            sends = tied[1:]
        for send, hops in zip(sends, due):
            odd = hops[0] % 2
            pairs = [(i, i + 1) for i in range(odd, count - 1, 2)]
            got = lax.ppermute(send, "seq", pairs + [(b, a) for a, b in pairs])
            for hop in hops:
                arrivals[stage - hop].append(got)
    grad_weight, grad_logits = call(
        functools.partial(weight_kernel, nv), "weight", (*[a[6] for a in firsts], hidden),
        (((value_heads, model_width), f32), ((value_heads, tokens), f32)), work // 4,
    )
    here = lax.axis_index("head")
    half = model_width // 2
    swap = [(0, 1), (1, 0)]
    weight_here = lax.dynamic_slice_in_dim(weight, here * half, half, 1)
    weight_there = lax.dynamic_slice_in_dim(weight, (1 - here) * half, half, 1)
    other_weight = lax.ppermute(weight_there, "head", swap)
    other_logits = lax.ppermute(grad_logits, "head", swap)
    seconds = []
    rounds = [
        (axis, 1 << n) for axis in ("dp", "seq") for n in range((lax.axis_size(axis) - 1).bit_length())
    ]
    for part in range(parts):
        _, _, n, r, s, e, small = firsts[part]
        if part:
            small, grad_weight = lax.optimization_barrier((small, grad_weight))
        for axis, step in rounds[part :] if part == parts - 1 else rounds[part : part + 1]:
            grad_weight = exchanged(grad_weight, axis, step)
        seconds.append(
            call(
                keys_kernel, "keys", (q[part], k[part], d[part], rows[part], cols[part], n, r, s, e, small),
                ((narrow, bf16), (narrow, bf16), ((tokens, nv), f32)), 20 * work,
            )
        )
    finals = (
        ((tokens, value_heads, value_dim), bf16), ((tokens, value_heads, value_dim), bf16),
        ((tokens, key_heads, key_dim), bf16), ((tokens, key_heads, key_dim), bf16),
        ((tokens, half), bf16), ((value_heads, tokens), f32),
    )
    attended, grad_values, grad_query, grad_key, grad_hidden, grad_gate = call(
        functools.partial(finish_kernel, parts), "finish",
        (
            grad_logits, other_logits, weight_here, other_weight,
            *[a[0] for a in firsts], *[a[1] for a in firsts],
            *[a[0] for a in seconds], *[a[1] for a in seconds], *[a[2] for a in seconds],
        ),
        finals, work, far_outs=range(5),
        scratch=[pltpu.VMEM(shape, kind) for shape, kind in finals[:5]]
        + [pltpu.VMEM((tokens * value_heads, value_dim), f32), pltpu.SemaphoreType.DMA((5,))],
    )
    return (
        attended[None], grad_query[None], grad_key[None], grad_values[None], grad_gate.T[None],
        grad_hidden[None], grad_weight.T,
    )


def solution(mesh):
    heads = P("dp", "seq", "head", None)
    return jax.shard_map(
        on_device,
        mesh=mesh,
        in_specs=(
            heads, heads, heads, P("dp", "seq", None), P(None, "head"), P("head"),
            P("dp", "seq", "head"), heads,
        ),
        out_specs=(
            heads, heads, heads, heads, P("dp", "seq", "head"), P("dp", "seq", "head"), P(None, "head"),
        ),
        check_vma=False,
    )
```

```python
import functools

import jax
import jax.numpy as jnp
from jax import lax
from jax.experimental import pallas as pl
from jax.experimental.pallas import tpu as pltpu
from jax.sharding import PartitionSpec as P

SUB = 128
KEY_GROUP = 2
VMEM = 24 * 1024 * 1024
WHOLE = 56 * 1024 * 1024
STORE = 68 * 1024 * 1024

eps_norm = 1e-06
f32 = jnp.float32
bf16 = jnp.bfloat16


def split(x):
    high = x.astype(bf16)
    return high, (x - high.astype(f32)).astype(bf16)


def dot(a, b, ca=1, cb=0):
    return lax.dot_general(a, b, (((ca,), (cb,)), ((), ())), preferred_element_type=f32)


def cat(parts, axis):
    return jnp.concatenate(parts, axis=axis)


def halves(x):
    width = x.shape[1] // 2
    return x[:, :width] + x[:, width:]


def square_product(a, b):
    ah, al = split(a)
    bh, bl = split(b)
    wide = cat([bh, bl], 1)
    return halves(dot(cat([ah, al], 1), cat([wide, wide], 0)))


def square_product_t(a, b):
    ah, al = split(a)
    bh, bl = split(b)
    wide = cat([bh, bl], 1)
    return halves(dot(cat([ah, al], 0), cat([wide, wide], 0), 0, 0))


def square_product_bt(a, b):
    ah, al = split(a)
    bh, bl = split(b)
    tall = cat([bh, bl], 0)
    return halves(dot(cat([ah, al], 1), cat([tall, tall], 1), 1, 1))


def positions(count):
    shape = (count, count)
    return (lax.broadcasted_iota(jnp.int32, shape, 0), lax.broadcasted_iota(jnp.int32, shape, 1))


def inverses(blocks):
    count = blocks[0].shape[0]
    row, column = positions(count)
    identity = jnp.where(row == column, 1.0, 0.0)
    found = None
    width = 1
    while width < count:
        pairs = (row // (2 * width) == column // (2 * width)) & (row // width != column // width)
        offs = [jnp.where(pairs, block, 0.0) for block in blocks]
        if found is None:
            found = [identity - off for off in offs]
        else:
            firsts = [square_product(inverse, off) for inverse, off in zip(found, offs)]
            found = [
                inverse - square_product(first, inverse) for first, inverse in zip(firsts, found)
            ]
        width *= 2
    return found


def unit_scales(raw, factor):
    data = raw.astype(f32)
    total = jnp.sum(data * data, axis=1, keepdims=True) + eps_norm
    return lax.rsqrt(total) * factor, total


def as_row(column):
    return jnp.transpose(jnp.broadcast_to(column, (column.shape[0], SUB)))[0:1, :]


def chunk_matrices(kr, qr):
    rk, sk = unit_scales(kr, 1.0)
    rq, sq = unit_scales(qr, kr.shape[1] ** (-0.5))
    rk_row = as_row(rk)
    both = dot(cat([kr, qr], 0), kr, 1, 1) * rk_row
    count = kr.shape[0]
    return rk, sk, rq, sq, rk_row, both[:count] * rk, both[count:] * rq


def decay_matrix(g_col, g_row, lower):
    return jnp.exp(jnp.where(lower, g_col - g_row, -1e30))


def before_kernel(part, key_count, place_ref, heads_ref, rows_ref, *refs):
    store_ref, m_ref, first_ref, held, sems, heads_held, heads_sem = refs[-7:]
    value_count = first_ref.shape[0]
    count = heads_held.shape[1]
    fetched, (q_ref, k_ref, v_ref, d_ref) = heads_of(
        part, key_count, value_count, heads_ref, heads_held, heads_sem
    )
    share = value_count // key_count
    row, column = positions(count)
    lower = row >= column
    strict = row > column
    rows = rows_ref[...]
    cols = jnp.transpose(rows)
    scales, mixings, systems = [], [], []
    fetched.wait()
    for i in range(key_count):
        kr, qr = k_ref[i], q_ref[i]
        rk, sk, rq, sq, rk_row, key_key, query_key = chunk_matrices(kr, qr)
        for r in range(share):
            h = i * share + r
            g_col, beta = cols[:, h : h + 1], cols[:, value_count + h : value_count + h + 1]
            decay = decay_matrix(g_col, rows[h : h + 1, :], lower)
            systems.append(jnp.where(strict, beta * decay * key_key, 0.0))
            mixings.append(decay * query_key)
            scales.append((rk, rq, beta, g_col))
    pieces = count // SUB
    diagonal = []
    for a in systems:
        for n in range(pieces):
            diagonal.append(a[n * SUB : (n + 1) * SUB, n * SUB : (n + 1) * SUB])
    diagonal = inverses(diagonal)
    identity = jnp.where(positions(SUB)[0] == positions(SUB)[1], 1.0, 0.0)
    copies = []

    def leave(n):
        size = 2 * value_count
        here = pl.ds(n * size, size)
        there = pl.ds((2 * part + n) * size, size)
        copies.append(pltpu.make_async_copy(held.at[here], store_ref.at[there], sems.at[n]))
        copies[-1].start()

    for h in range(value_count):
        a = systems[h]
        blocks = [[None] * pieces for _ in range(pieces)]
        for n in range(pieces):
            blocks[n][n] = diagonal[h * pieces + n]
            for m in range(n):
                total = None
                for l in range(m, n):
                    term = square_product(
                        a[n * SUB : (n + 1) * SUB, l * SUB : (l + 1) * SUB], blocks[l][m]
                    )
                    total = term if total is None else total + term
                blocks[n][m] = -square_product(blocks[n][n], total)
            for m in range(n + 1, pieces):
                blocks[n][m] = jnp.zeros((SUB, SUB), f32)
        held[h], held[value_count + h] = split(cat([cat(line, 1) for line in blocks], 0))
    leave(0)
    for h in range(value_count):
        rk, rq, beta, g_col = scales[h]
        kr, qr, v, d = k_ref[h // share], q_ref[h // share], v_ref[h], d_ref[h]
        width = kr.shape[1]
        last = g_col[count - 1 : count, :]
        growth = jnp.exp(g_col)
        to_end = jnp.exp(last - g_col) * rk
        ph, pl_ = split(mixings[h])
        pulled = dot(ph, d, 0, 0) + dot(pl_, d, 0, 0)
        th, tl = held[h], held[value_count + h]
        keys_h, keys_l = split(to_end * kr.astype(f32))
        pull_h, pull_l = split(pulled)
        high = dot(th, cat([keys_h, pull_h, keys_l, pull_l], 1), 0, 0)
        yz = high[:, : 2 * width] + high[:, 2 * width :]
        yz = yz + dot(tl, cat([keys_h, pull_h], 1), 0, 0)
        y, z = yz[:, :width], yz[:, width:]
        held[2 * value_count + h], held[3 * value_count + h] = split(yz)
        yb = y * beta
        bh, bl = split(yb)
        base = dot(bh, v, 0, 0) + dot(bl, v, 0, 0)
        mh, ml = split(yb * (growth * rk))
        m_ref[h] = identity * jnp.exp(last) - (dot(mh, kr, 0, 0) + dot(ml, kr, 0, 0))
        outs_h, outs_l = split((growth * rq) * d.astype(f32))
        ins_h, ins_l = split((beta * growth * rk) * z)
        push = halves(
            dot(qr, cat([outs_h, outs_l], 1), 0, 0) - dot(kr, cat([ins_h, ins_l], 1), 0, 0)
        )
        m_ref[value_count + h] = base
        m_ref[2 * value_count + h] = push
        first_ref[h] = jnp.where(place_ref[0] == 0, base, push)
    leave(1)
    for copy in copies:
        copy.wait()


def relay_kernel(hops, count, place_ref, *refs):
    place, out_ref = place_ref[0], refs[-1]
    at = 0
    for hop in hops:
        if hop == 0:
            first_ref = refs[at]
            at += 1

            @pl.when((place == 0) | (place == count - 1))
            def _():
                out_ref[...] = first_ref[...]

            continue
        parts_ref, got_ref = refs[at : at + 2]
        heads = got_ref.shape[0]
        at += 2

        @pl.when(place == hop)
        def _():
            for h in range(heads):
                out_ref[h] = square_product(parts_ref[h], got_ref[h]) + parts_ref[heads + h]

        @pl.when(place == count - 1 - hop)
        def _():
            for h in range(heads):
                out_ref[h] = square_product_t(parts_ref[h], got_ref[h]) + parts_ref[2 * heads + h]


def chosen(place, arrivals, h, first, step):
    total = jnp.zeros(arrivals[0].shape[1:], f32)
    for hop, arrival in enumerate(arrivals):
        total = jnp.where(first + step * place == hop, arrival[h], total)
    return total


def values_kernel(part, key_count, *refs):
    place_ref, heads_ref, rows_ref, store_ref = refs[:4]
    arrivals = refs[4:-11]
    o_ref, dv_ref, n_ref, r_ref, s_ref, e_ref, small_ref, held, sems, heads_held, heads_sem = refs[-11:]
    value_count, count, width = o_ref.shape
    fetched, (q_ref, k_ref, v_ref, d_ref) = heads_of(
        part, key_count, value_count, heads_ref, heads_held, heads_sem
    )
    share = value_count // key_count
    size = 2 * value_count
    copies = [
        pltpu.make_async_copy(
            store_ref.at[pl.ds((2 * part + n) * size, size)], held.at[pl.ds(n * size, size)], sems.at[n]
        )
        for n in range(2)
    ]
    for copy in copies:
        copy.start()
    row, column = positions(count)
    lower = row >= column
    rows = rows_ref[...]
    cols = jnp.transpose(rows)
    place = place_ref[0]
    ready = []
    fetched.wait()
    for i in range(key_count):
        kr, qr = k_ref[i], q_ref[i]
        rk, _ = unit_scales(kr, 1.0)
        rq, _ = unit_scales(qr, width ** (-0.5))
        query_key = dot(qr, kr, 1, 1) * as_row(rk) * rq
        both = cat([qr, kr], 0)
        for r in range(share):
            h = i * share + r
            g_col, beta = cols[:, h : h + 1], cols[:, value_count + h : value_count + h + 1]
            decay = decay_matrix(g_col, rows[h : h + 1, :], lower)
            growth = jnp.exp(g_col)
            s = chosen(place, arrivals, h, -1, 1)
            e = chosen(place, arrivals, h, len(arrivals) - 1, -1)
            s_ref[h] = s
            e_ref[h] = e
            carried = halves(dot(both, cat(split(s), 1)))
            residual = beta * (v_ref[h].astype(f32) - (growth * rk) * carried[count:])
            ready.append(
                (split(residual), split(decay * query_key), (growth * rq) * carried[:count], beta, split(e))
            )
    for copy in copies:
        copy.wait()
    gates, logits = [], []
    for h, ((rh, rl), (ph, pl_), from_state, beta, (eh, el)) in enumerate(ready):
        th, tl = held[h], held[value_count + h]
        yzh, yzl = held[2 * value_count + h], held[3 * value_count + h]
        new = halves(dot(th, cat([rh, rl], 1))) + dot(tl, rh)
        n_ref[h] = new
        nh, nl = split(new)
        out = from_state + halves(dot(ph, cat([nh, nl], 1))) + dot(pl_, nh)
        o_ref[h] = out.astype(bf16)
        wide = cat([eh, el], 1)
        pulled = halves(dot(cat([yzh[:, :width], yzl[:, :width]], 1), cat([wide, wide], 0)))
        d_res = yzh[:, width:].astype(f32) + yzl[:, width:].astype(f32) + pulled
        r_ref[h] = d_res
        dv = beta * d_res
        dv_ref[h] = dv.astype(bf16)
        logits.append((1.0 - beta) * jnp.sum(d_res * new, axis=1, keepdims=True))
        gates.append(
            jnp.sum(d_ref[h].astype(f32) * out - dv * v_ref[h].astype(f32), axis=1, keepdims=True)
        )
    after = jnp.where(row <= column, 1.0, 0.0).astype(bf16)
    gh, gl = split(cat(gates, 1))
    small_ref[...] = cat([halves(dot(after, cat([gh, gl], 1)))] + logits, 1)


def keys_kernel(
    part, heads_ref, rows_ref, n_ref, r_ref, s_ref, e_ref, small_ref, dq_ref, dk_ref, gate_ref,
    heads_held, heads_sem,
):
    key_count, count, width = dq_ref.shape
    value_count = n_ref.shape[0]
    fetched, (q_ref, k_ref, _, d_ref) = heads_of(
        part, key_count, value_count, heads_ref, heads_held, heads_sem
    )
    share = value_count // key_count
    row, column = positions(count)
    lower = row >= column
    strict = row > column
    rows = rows_ref[...]
    cols = jnp.transpose(rows)
    gates = []
    fetched.wait()
    for i in range(key_count):
        kr, qr = k_ref[i], q_ref[i]
        kf, qf = kr.astype(f32), qr.astype(f32)
        rk, sk = unit_scales(kr, 1.0)
        rq, sq = unit_scales(qr, width ** (-0.5))
        rk_row = as_row(rk)
        mix_grad = pair_grad = dq = dk = None
        for r in range(share):
            h = i * share + r
            g_col, beta = cols[:, h : h + 1], cols[:, value_count + h : value_count + h + 1]
            decay = decay_matrix(g_col, rows[h : h + 1, :], lower)
            growth = jnp.exp(g_col)
            last = g_col[count - 1 : count, :]
            to_end = jnp.exp(last - g_col)
            d = d_ref[h]
            s, e, new, d_res = s_ref[h], e_ref[h], n_ref[h], r_ref[h]
            sh, sl = split(s)
            nh, nl = split(new)
            drh, drl = split(d_res)
            tall = cat([nh, nl], 1)
            d_mix = dot(cat([d, d], 1), tall, 1, 1)
            d_sys = dot(cat([drh, drh], 1), tall, 1, 1) + dot(drl, nh, 1, 1)
            term = decay * d_mix
            mix_grad = term if mix_grad is None else mix_grad + term
            term = jnp.where(strict, beta * decay * d_sys, 0.0)
            pair_grad = term if pair_grad is None else pair_grad + term
            term = growth * dot(cat([d, d], 1), cat([sh, sl], 1), 1, 1)
            dq = term if dq is None else dq + term
            from_end = to_end * square_product_bt(new, e)
            from_in = (growth * beta) * square_product_bt(d_res, s)
            total = jnp.sum(from_end * kf * rk, axis=0, keepdims=True) + jnp.exp(last) * jnp.sum(
                s * e, axis=0, keepdims=True
            )
            gates.append(jnp.sum(total, axis=1, keepdims=True))
            term = from_end - from_in
            dk = term if dk is None else dk + term
        mh, ml = split(mix_grad * rk_row)
        dq = dq + dot(mh, kr) + dot(ml, kr)
        xh, xl = split(mix_grad * rq)
        dk = dk + dot(xh, qr, 0, 0) + dot(xl, qr, 0, 0)
        gh, gl = split(pair_grad * rk_row)
        dk = dk - (dot(gh, kr) + dot(gl, kr))
        gh, gl = split(pair_grad * rk)
        dk = dk - (dot(gh, kr, 0, 0) + dot(gl, kr, 0, 0))
        along = jnp.sum(qf * dq, axis=1, keepdims=True)
        dq_ref[i] = (rq * (dq - qf * (along / sq))).astype(bf16)
        along = jnp.sum(kf * dk, axis=1, keepdims=True)
        dk_ref[i] = (rk * (dk - kf * (along / sk))).astype(bf16)
    gate_ref[...] = small_ref[...][:, :value_count] + cat(gates, 1)


def call(kernel, name, operands, outs, flops, far_ins=(), far_outs=(), scratch=(), limit=VMEM, same=None):
    def spec(n, kind, far):
        space = pltpu.SMEM if kind == jnp.int32 else pltpu.HBM if n in far else pltpu.VMEM
        return pl.BlockSpec(memory_space=space)

    return pl.pallas_call(
        kernel,
        name=name,
        in_specs=[spec(n, x.dtype, far_ins) for n, x in enumerate(operands)],
        out_specs=[spec(n, kind, far_outs) for n, (_, kind) in enumerate(outs)],
        out_shape=[jax.ShapeDtypeStruct(shape, kind) for shape, kind in outs],
        scratch_shapes=list(scratch),
        input_output_aliases=same or {},
        compiler_params=pltpu.CompilerParams(vmem_limit_bytes=limit),
        cost_estimate=pl.CostEstimate(flops=flops, bytes_accessed=1 << 20, transcendentals=0),
    )(*operands)


def turned(parts):
    count = sum(part.shape[1] for part in parts)
    filler = jnp.zeros((parts[0].shape[0], SUB - count), f32)
    return jnp.transpose(cat(parts + [filler], 1))[:count]


def arrange_kernel(nk, nv, *refs):
    store_ref, outs = refs[8], refs[9:-11]
    inputs, made, sems, out_sems = refs[-11:-3], refs[-3], refs[-2], refs[-1]
    held = inputs
    copies = [
        pltpu.make_async_copy(ref, into, sems.at[n]) for n, (ref, into) in enumerate(zip(refs[:8], held))
    ]
    for copy in copies:
        copy.start()
    size = 2 * (nk + nv)
    firsts = (0, nk, 2 * nk, 2 * nk + nv)
    leaving = []
    parts = len(outs)
    copies[0].wait()
    rates = held[0][...]
    heads = rates.shape[0]
    high, low = split(rates)
    rest = (rates - high.astype(f32) - low.astype(f32)).astype(bf16)
    row, column = positions(rates.shape[1])
    before = jnp.where(row <= column, 1.0, 0.0).astype(bf16)
    sums = dot(cat([high, low, rest], 0), before)
    summed = sums[:heads] + sums[heads : 2 * heads] + sums[2 * heads :]
    for n in range(4):
        copies[3 + n].wait()
        ref = held[3 + n]
        count, each, width = ref.shape
        group = each // parts
        for part in range(parts):
            turn = jnp.swapaxes(ref[:, part * group : (part + 1) * group, :].astype(f32), 0, 1)
            here = pl.ds(part * size + firsts[n], group)
            made[here] = turn.astype(bf16)
            leaving.append(
                pltpu.make_async_copy(made.at[here], store_ref.at[here], out_sems.at[n * parts + part])
            )
            leaving[-1].start()
    for n in (1, 2, 7):
        copies[n].wait()
    row, column = positions(heads)
    bias = jnp.sum(jnp.where(row == column, held[1][...], 0.0), axis=1, keepdims=True)
    beta = jax.nn.sigmoid(dot(held[2][...], held[7][...], 1, 1) + bias)
    for part in range(parts):
        first = part * nv
        outs[part][...] = cat([summed[first : first + nv], beta[first : first + nv]], 0)
    for copy in leaving:
        copy.wait()


def heads_of(part, nk, nv, store_ref, held, sem):
    size = 2 * (nk + nv)
    copy = pltpu.make_async_copy(store_ref.at[pl.ds(part * size, size)], held, sem)
    copy.start()
    return copy, [held.at[pl.ds(n, m)] for n, m in ((0, nk), (nk, nk), (2 * nk, nv), (2 * nk + nv, nv))]


def weight_kernel(nv, *refs):
    smalls, (hidden_ref, part_ref, logit_ref) = refs[:-3], refs[-3:]
    rows = [turned([ref[n * SUB : (n + 1) * SUB, nv : 2 * nv] for ref in smalls]) for n in range(smalls[0].shape[0] // SUB)]
    rows = cat(rows, 1)
    logit_ref[...] = rows
    heads = rows.shape[0]
    both = dot(cat(split(rows), 0), hidden_ref[...])
    part_ref[...] = both[:heads] + both[heads:]


def finish_kernel(parts, *refs):
    logit_ref, other_ref, weight_ref, other_weight_ref = refs[:4]
    ins, outs, gate_ref = refs[4 : 4 + 5 * parts], refs[4 + 5 * parts : -8], refs[-8]
    held, wide_ref, sems = refs[-7:-2], refs[-2], refs[-1]
    copies = [
        pltpu.make_async_copy(held[n], outs[n], sems.at[n]) for n in range(5)
    ]
    for n in range(4):
        count, heads, width = held[n].shape
        group = heads // parts
        whole = cat([ref[...].astype(f32) for ref in ins[n * parts : (n + 1) * parts]], 0)
        held[n][...] = jnp.swapaxes(whole, 0, 1).astype(bf16)
        copies[n].start()
        if n == 1:
            high, low = split(cat([logit_ref[...], other_ref[...]], 0))
            weight = cat([weight_ref[...], other_weight_ref[...]], 0)
            held[4][...] = dot(cat([high, low], 0), cat([weight, weight], 0), 0, 0).astype(bf16)
            copies[4].start()
    gates = ins[4 * parts :]
    for n in range(gate_ref.shape[1] // SUB):
        here = slice(n * SUB, (n + 1) * SUB)
        gate_ref[:, here] = turned([ref[here, :] for ref in gates])
    for copy in copies:
        copy.wait()


def exchanged(value, axis, step):
    pairs = [(i, i ^ step) for i in range(lax.axis_size(axis))]
    return value + lax.ppermute(value, axis, pairs)


def on_device(queries, keys_in, values, hidden_in, beta_weight, beta_bias, log_gate, out_grad):
    _, tokens, model_width = hidden_in.shape
    key_heads, key_dim = queries.shape[2:]
    value_heads, value_dim = values.shape[2:]
    nk = KEY_GROUP
    nv = nk * value_heads // key_heads
    parts = key_heads // nk
    count = lax.axis_size("seq")
    place = lax.axis_index("seq").astype(jnp.int32).reshape(1)
    hidden = hidden_in.reshape(tokens, model_width)
    weight = beta_weight.T

    narrow = (nk, tokens, key_dim)
    chunk = (nv, tokens, value_dim)
    state = (nv, key_dim, value_dim)
    moves = (3 * nv, key_dim, value_dim)
    work = nv * 2 * tokens**3
    inputs = (
        log_gate[0].T, beta_bias.reshape(1, value_heads), weight,
        queries[0], keys_in[0], values[0], out_grad[0], hidden,
    )
    size = 2 * (nk + nv)
    stacked = (max(size * parts, STORE // (2 * tokens * key_dim)), tokens, key_dim)
    heads, *rows = call(
        functools.partial(arrange_kernel, nk, nv), "arrange", inputs,
        [(stacked, bf16)] + [((2 * nv, tokens), f32)] * parts,
        work, far_ins=range(len(inputs)), far_outs=(0,), limit=WHOLE,
        scratch=[pltpu.VMEM(x.shape, x.dtype) for x in inputs]
        + [
            pltpu.VMEM((size * parts, tokens, key_dim), bf16),
            pltpu.SemaphoreType.DMA((len(inputs),)), pltpu.SemaphoreType.DMA((4 * parts,)),
        ],
    )
    fetch = [pltpu.VMEM((size, tokens, key_dim), bf16), pltpu.SemaphoreType.DMA(())]
    length = max(4 * nv * parts, STORE // (2 * tokens * tokens))
    blocks = (length, tokens, tokens)
    held = [pltpu.VMEM((4 * nv, tokens, tokens), bf16), pltpu.SemaphoreType.DMA((2,))]

    def before(part):
        operands = (place, heads, rows[part])
        return call(
            functools.partial(before_kernel, part, nk), "before", operands + tuple(store),
            ((blocks, bf16), (moves, f32), (state, f32)),
            60 * work, far_ins=(1, len(operands)), far_outs=(0,), scratch=held + fetch,
            same={len(operands): 0} if store else None,
        )

    def relay(stage, hops, operands):
        for hop in hops:
            made = befores[stage - hop]
            operands = operands + ([made[1], arrivals[stage - hop][-1]] if hop else [made[2]])
        if hops == [0]:
            return operands[1]
        (send,) = call(
            functools.partial(relay_kernel, hops, count), "relay", operands, ((state, f32),), work // 4,
        )
        return send

    def new_values(part):
        return call(
            functools.partial(values_kernel, part, nk), "values",
            (place, heads, rows[part], *store, *arrivals[part]),
            (
                (chunk, bf16), (chunk, bf16), (chunk, f32), (chunk, f32), (state, f32), (state, f32),
                ((tokens, 2 * nv), f32),
            ),
            20 * work, far_ins=(1, 3), scratch=held + fetch,
        )

    befores, firsts, store, here = [], [], [], place
    arrivals = [[] for _ in range(parts)]
    shift = max(parts, count)
    for stage in range(shift + parts):
        if stage < parts:
            befores.append([*before(stage)])
            store[:] = befores[stage][:1]
            here, befores[stage][2] = lax.optimization_barrier((place, befores[stage][2]))
        elif stage >= shift:
            firsts.append([*new_values(stage - shift)])
            here, firsts[-1][6] = lax.optimization_barrier((place, firsts[-1][6]))
        due = [hop for hop in range(count - 1) if 0 <= stage - hop < parts]
        due = [hops for hops in ([h for h in due if not h % 2], [h for h in due if h % 2]) if hops]
        sends = [relay(stage, hops, [here]) for hops in due]
        following = stage + 1 if stage + 1 < parts else stage + 1 - shift
        if sends and 0 <= following < parts:
            tied = lax.optimization_barrier((rows[following], *sends))
            rows[following] = tied[0]
            sends = tied[1:]
        for send, hops in zip(sends, due):
            odd = hops[0] % 2
            pairs = [(i, i + 1) for i in range(odd, count - 1, 2)]
            got = lax.ppermute(send, "seq", pairs + [(b, a) for a, b in pairs])
            for hop in hops:
                arrivals[stage - hop].append(got)
    grad_weight, grad_logits = call(
        functools.partial(weight_kernel, nv), "weight", (*[a[6] for a in firsts], hidden),
        (((value_heads, model_width), f32), ((value_heads, tokens), f32)), work // 4,
    )
    here = lax.axis_index("head")
    half = model_width // 2
    swap = [(0, 1), (1, 0)]
    weight_here = lax.dynamic_slice_in_dim(weight, here * half, half, 1)
    weight_there = lax.dynamic_slice_in_dim(weight, (1 - here) * half, half, 1)
    other_weight = lax.ppermute(weight_there, "head", swap)
    other_logits = lax.ppermute(grad_logits, "head", swap)
    seconds = []
    rounds = [
        (axis, 1 << n) for axis in ("dp", "seq") for n in range((lax.axis_size(axis) - 1).bit_length())
    ]
    for part in range(parts):
        _, _, n, r, s, e, small = firsts[part]
        if part:
            small, grad_weight = lax.optimization_barrier((small, grad_weight))
        for axis, step in rounds[part :] if part == parts - 1 else rounds[part : part + 1]:
            grad_weight = exchanged(grad_weight, axis, step)
        seconds.append(
            call(
                functools.partial(keys_kernel, part), "keys", (heads, rows[part], n, r, s, e, small),
                ((narrow, bf16), (narrow, bf16), ((tokens, nv), f32)), 20 * work, far_ins=(0,), scratch=fetch,
            )
        )
    finals = (
        ((tokens, value_heads, value_dim), bf16), ((tokens, value_heads, value_dim), bf16),
        ((tokens, key_heads, key_dim), bf16), ((tokens, key_heads, key_dim), bf16),
        ((tokens, half), bf16), ((value_heads, tokens), f32),
    )
    attended, grad_values, grad_query, grad_key, grad_hidden, grad_gate = call(
        functools.partial(finish_kernel, parts), "finish",
        (
            grad_logits, other_logits, weight_here, other_weight,
            *[a[0] for a in firsts], *[a[1] for a in firsts],
            *[a[0] for a in seconds], *[a[1] for a in seconds], *[a[2] for a in seconds],
        ),
        finals, work, far_outs=range(5),
        scratch=[pltpu.VMEM(shape, kind) for shape, kind in finals[:5]]
        + [pltpu.VMEM((tokens * value_heads, value_dim), f32), pltpu.SemaphoreType.DMA((5,))],
    )
    return (
        attended[None], grad_query[None], grad_key[None], grad_values[None], grad_gate.T[None],
        grad_hidden[None], grad_weight.T,
    )


def solution(mesh):
    heads = P("dp", "seq", "head", None)
    return jax.shard_map(
        on_device,
        mesh=mesh,
        in_specs=(
            heads, heads, heads, P("dp", "seq", None), P(None, "head"), P("head"),
            P("dp", "seq", "head"), heads,
        ),
        out_specs=(
            heads, heads, heads, heads, P("dp", "seq", "head"), P("dp", "seq", "head"), P(None, "head"),
        ),
        check_vma=False,
    )
```

```python
import functools

import jax
import jax.numpy as jnp
from jax import lax
from jax.experimental import pallas as pl
from jax.experimental.pallas import tpu as pltpu
from jax.sharding import PartitionSpec as P

SUB = 128
KEY_GROUP = 2
OWN_FETCH = (1,)
VMEM = 24 * 1024 * 1024
WHOLE = 56 * 1024 * 1024
STORE = 68 * 1024 * 1024

eps_norm = 1e-06
f32 = jnp.float32
bf16 = jnp.bfloat16


def split(x):
    high = x.astype(bf16)
    return high, (x - high.astype(f32)).astype(bf16)


def dot(a, b, ca=1, cb=0):
    return lax.dot_general(a, b, (((ca,), (cb,)), ((), ())), preferred_element_type=f32)


def cat(parts, axis):
    return jnp.concatenate(parts, axis=axis)


def halves(x):
    width = x.shape[1] // 2
    return x[:, :width] + x[:, width:]


def square_product(a, b):
    ah, al = split(a)
    bh, bl = split(b)
    wide = cat([bh, bl], 1)
    return halves(dot(cat([ah, al], 1), cat([wide, wide], 0)))


def square_product_t(a, b):
    ah, al = split(a)
    bh, bl = split(b)
    wide = cat([bh, bl], 1)
    return halves(dot(cat([ah, al], 0), cat([wide, wide], 0), 0, 0))


def square_product_bt(a, b):
    ah, al = split(a)
    bh, bl = split(b)
    tall = cat([bh, bl], 0)
    return halves(dot(cat([ah, al], 1), cat([tall, tall], 1), 1, 1))


def positions(count):
    shape = (count, count)
    return (lax.broadcasted_iota(jnp.int32, shape, 0), lax.broadcasted_iota(jnp.int32, shape, 1))


def inverses(blocks):
    count = blocks[0].shape[0]
    row, column = positions(count)
    identity = jnp.where(row == column, 1.0, 0.0)
    found = None
    width = 1
    while width < count:
        pairs = (row // (2 * width) == column // (2 * width)) & (row // width != column // width)
        offs = [jnp.where(pairs, block, 0.0) for block in blocks]
        if found is None:
            found = [identity - off for off in offs]
        else:
            firsts = [square_product(inverse, off) for inverse, off in zip(found, offs)]
            found = [
                inverse - square_product(first, inverse) for first, inverse in zip(firsts, found)
            ]
        width *= 2
    return found


def unit_scales(raw, factor):
    data = raw.astype(f32)
    total = jnp.sum(data * data, axis=1, keepdims=True) + eps_norm
    return lax.rsqrt(total) * factor, total


def as_row(column):
    return jnp.transpose(jnp.broadcast_to(column, (column.shape[0], SUB)))[0:1, :]


def chunk_matrices(kr, qr):
    rk, sk = unit_scales(kr, 1.0)
    rq, sq = unit_scales(qr, kr.shape[1] ** (-0.5))
    rk_row = as_row(rk)
    both = dot(cat([kr, qr], 0), kr, 1, 1) * rk_row
    count = kr.shape[0]
    return rk, sk, rq, sq, rk_row, both[:count] * rk, both[count:] * rq


def decay_matrix(g_col, g_row, lower):
    return jnp.exp(jnp.where(lower, g_col - g_row, -1e30))


def before_kernel(part, parts, key_count, place_ref, heads_ref, rows_ref, *refs):
    if part:
        mine_ref = refs[0]
        refs = refs[2:]
    else:
        mine_ref = refs[-1]
        refs = refs[:-1]
    store_ref, m_ref, first_ref, ahead_ref = refs[:4]
    held, sems = refs[-2:]
    value_count = first_ref.shape[0]
    count = mine_ref.shape[1]
    if part == 0:
        part_of(part, heads_ref, mine_ref, sems.at[2]).wait()
    coming = [part_of((part + 1) % parts, heads_ref, ahead_ref, sems.at[3])]
    if part == parts - 1:
        coming.append(part_of(0, store_ref, refs[4], sems.at[4]))
    q_ref, k_ref, v_ref, d_ref = heads_of(key_count, value_count, mine_ref)
    share = value_count // key_count
    row, column = positions(count)
    lower = row >= column
    strict = row > column
    rows = rows_ref[...]
    cols = jnp.transpose(rows)
    scales, mixings, systems = [], [], []
    for i in range(key_count):
        kr, qr = k_ref[i], q_ref[i]
        rk, sk, rq, sq, rk_row, key_key, query_key = chunk_matrices(kr, qr)
        for r in range(share):
            h = i * share + r
            g_col, beta = cols[:, h : h + 1], cols[:, value_count + h : value_count + h + 1]
            decay = decay_matrix(g_col, rows[h : h + 1, :], lower)
            systems.append(jnp.where(strict, beta * decay * key_key, 0.0))
            mixings.append(decay * query_key)
            scales.append((rk, rq, beta, g_col))
    pieces = count // SUB
    diagonal = []
    for a in systems:
        for n in range(pieces):
            diagonal.append(a[n * SUB : (n + 1) * SUB, n * SUB : (n + 1) * SUB])
    diagonal = inverses(diagonal)
    identity = jnp.where(positions(SUB)[0] == positions(SUB)[1], 1.0, 0.0)
    copies = []

    def leave(n):
        size = 2 * value_count
        here = pl.ds(n * size, size)
        there = pl.ds((2 * part + n) * size, size)
        copies.append(pltpu.make_async_copy(held.at[here], store_ref.at[there], sems.at[n]))
        copies[-1].start()

    for h in range(value_count):
        a = systems[h]
        blocks = [[None] * pieces for _ in range(pieces)]
        for n in range(pieces):
            blocks[n][n] = diagonal[h * pieces + n]
            for m in range(n):
                total = None
                for l in range(m, n):
                    term = square_product(
                        a[n * SUB : (n + 1) * SUB, l * SUB : (l + 1) * SUB], blocks[l][m]
                    )
                    total = term if total is None else total + term
                blocks[n][m] = -square_product(blocks[n][n], total)
            for m in range(n + 1, pieces):
                blocks[n][m] = jnp.zeros((SUB, SUB), f32)
        held[h], held[value_count + h] = split(cat([cat(line, 1) for line in blocks], 0))
    leave(0)
    for h in range(value_count):
        rk, rq, beta, g_col = scales[h]
        kr, qr, v, d = k_ref[h // share], q_ref[h // share], v_ref[h], d_ref[h]
        width = kr.shape[1]
        last = g_col[count - 1 : count, :]
        growth = jnp.exp(g_col)
        to_end = jnp.exp(last - g_col) * rk
        ph, pl_ = split(mixings[h])
        pulled = dot(ph, d, 0, 0) + dot(pl_, d, 0, 0)
        th, tl = held[h], held[value_count + h]
        keys_h, keys_l = split(to_end * kr.astype(f32))
        pull_h, pull_l = split(pulled)
        high = dot(th, cat([keys_h, pull_h, keys_l, pull_l], 1), 0, 0)
        yz = high[:, : 2 * width] + high[:, 2 * width :]
        yz = yz + dot(tl, cat([keys_h, pull_h], 1), 0, 0)
        y, z = yz[:, :width], yz[:, width:]
        held[2 * value_count + h], held[3 * value_count + h] = split(yz)
        yb = y * beta
        bh, bl = split(yb)
        base = dot(bh, v, 0, 0) + dot(bl, v, 0, 0)
        mh, ml = split(yb * (growth * rk))
        m_ref[h] = identity * jnp.exp(last) - (dot(mh, kr, 0, 0) + dot(ml, kr, 0, 0))
        outs_h, outs_l = split((growth * rq) * d.astype(f32))
        ins_h, ins_l = split((beta * growth * rk) * z)
        push = halves(
            dot(qr, cat([outs_h, outs_l], 1), 0, 0) - dot(kr, cat([ins_h, ins_l], 1), 0, 0)
        )
        m_ref[value_count + h] = base
        m_ref[2 * value_count + h] = push
        first_ref[h] = jnp.where(place_ref[0] == 0, base, push)
    leave(1)
    for copy in copies + coming:
        copy.wait()


def relay_kernel(hops, count, place_ref, *refs):
    place, out_ref = place_ref[0], refs[-1]
    at = 0
    for hop in hops:
        if hop == 0:
            first_ref = refs[at]
            at += 1

            @pl.when((place == 0) | (place == count - 1))
            def _():
                out_ref[...] = first_ref[...]

            continue
        parts_ref, got_ref = refs[at : at + 2]
        heads = got_ref.shape[0]
        at += 2

        @pl.when(place == hop)
        def _():
            for h in range(heads):
                out_ref[h] = square_product(parts_ref[h], got_ref[h]) + parts_ref[heads + h]

        @pl.when(place == count - 1 - hop)
        def _():
            for h in range(heads):
                out_ref[h] = square_product_t(parts_ref[h], got_ref[h]) + parts_ref[2 * heads + h]


def chosen(place, arrivals, h, first, step):
    total = jnp.zeros(arrivals[0].shape[1:], f32)
    for hop, arrival in enumerate(arrivals):
        total = jnp.where(first + step * place == hop, arrival[h], total)
    return total


def values_kernel(part, parts, key_count, *refs):
    place_ref, heads_ref, rows_ref, store_ref, mine_ref = refs[:5]
    own, other = part in OWN_FETCH, part + 1 < parts and part + 1 not in OWN_FETCH
    if own:
        held, refs = refs[-1], refs[5:-1]
    else:
        held, refs = refs[5], refs[6:]
    outs = 9 if other else 8
    arrivals = refs[: -outs - 1]
    o_ref, dv_ref, n_ref, r_ref, s_ref, e_ref, small_ref, ahead_ref = refs[-outs - 1 :][:8]
    sems = refs[-1]
    value_count, count, width = o_ref.shape
    if own:
        fetched = part_of(part, store_ref, held, sems.at[2])
    coming = [part_of((part + 1) % parts, heads_ref, ahead_ref, sems.at[0])]
    if other:
        coming.append(part_of(part + 1, store_ref, refs[-2], sems.at[1]))
    q_ref, k_ref, v_ref, d_ref = heads_of(key_count, value_count, mine_ref)
    share = value_count // key_count
    row, column = positions(count)
    lower = row >= column
    rows = rows_ref[...]
    cols = jnp.transpose(rows)
    place = place_ref[0]
    ready = []
    for i in range(key_count):
        kr, qr = k_ref[i], q_ref[i]
        rk, _ = unit_scales(kr, 1.0)
        rq, _ = unit_scales(qr, width ** (-0.5))
        query_key = dot(qr, kr, 1, 1) * as_row(rk) * rq
        both = cat([qr, kr], 0)
        for r in range(share):
            h = i * share + r
            g_col, beta = cols[:, h : h + 1], cols[:, value_count + h : value_count + h + 1]
            decay = decay_matrix(g_col, rows[h : h + 1, :], lower)
            growth = jnp.exp(g_col)
            s = chosen(place, arrivals, h, -1, 1)
            e = chosen(place, arrivals, h, len(arrivals) - 1, -1)
            s_ref[h] = s
            e_ref[h] = e
            carried = halves(dot(both, cat(split(s), 1)))
            residual = beta * (v_ref[h].astype(f32) - (growth * rk) * carried[count:])
            ready.append(
                (split(residual), split(decay * query_key), (growth * rq) * carried[:count], beta, split(e))
            )
    if own:
        fetched.wait()
    gates, logits = [], []
    for h, ((rh, rl), (ph, pl_), from_state, beta, (eh, el)) in enumerate(ready):
        th, tl = held[h], held[value_count + h]
        yzh, yzl = held[2 * value_count + h], held[3 * value_count + h]
        new = halves(dot(th, cat([rh, rl], 1))) + dot(tl, rh)
        n_ref[h] = new
        nh, nl = split(new)
        out = from_state + halves(dot(ph, cat([nh, nl], 1))) + dot(pl_, nh)
        o_ref[h] = out.astype(bf16)
        wide = cat([eh, el], 1)
        pulled = halves(dot(cat([yzh[:, :width], yzl[:, :width]], 1), cat([wide, wide], 0)))
        d_res = yzh[:, width:].astype(f32) + yzl[:, width:].astype(f32) + pulled
        r_ref[h] = d_res
        dv = beta * d_res
        dv_ref[h] = dv.astype(bf16)
        logits.append((1.0 - beta) * jnp.sum(d_res * new, axis=1, keepdims=True))
        gates.append(
            jnp.sum(d_ref[h].astype(f32) * out - dv * v_ref[h].astype(f32), axis=1, keepdims=True)
        )
    after = jnp.where(row <= column, 1.0, 0.0).astype(bf16)
    gh, gl = split(cat(gates, 1))
    small_ref[...] = cat([halves(dot(after, cat([gh, gl], 1)))] + logits, 1)
    for copy in coming:
        copy.wait()


def keys_kernel(
    part, parts, heads_ref, rows_ref, mine_ref, n_ref, r_ref, s_ref, e_ref, small_ref,
    dq_ref, dk_ref, gate_ref, *ahead,
):
    key_count, count, width = dq_ref.shape
    value_count = n_ref.shape[0]
    coming = [part_of(part + 1, heads_ref, *ahead)] if part < parts - 1 else []
    q_ref, k_ref, _, d_ref = heads_of(key_count, value_count, mine_ref)
    share = value_count // key_count
    row, column = positions(count)
    lower = row >= column
    strict = row > column
    rows = rows_ref[...]
    cols = jnp.transpose(rows)
    gates = []
    for i in range(key_count):
        kr, qr = k_ref[i], q_ref[i]
        kf, qf = kr.astype(f32), qr.astype(f32)
        rk, sk = unit_scales(kr, 1.0)
        rq, sq = unit_scales(qr, width ** (-0.5))
        rk_row = as_row(rk)
        mix_grad = pair_grad = dq = dk = None
        for r in range(share):
            h = i * share + r
            g_col, beta = cols[:, h : h + 1], cols[:, value_count + h : value_count + h + 1]
            decay = decay_matrix(g_col, rows[h : h + 1, :], lower)
            growth = jnp.exp(g_col)
            last = g_col[count - 1 : count, :]
            to_end = jnp.exp(last - g_col)
            d = d_ref[h]
            s, e, new, d_res = s_ref[h], e_ref[h], n_ref[h], r_ref[h]
            sh, sl = split(s)
            nh, nl = split(new)
            drh, drl = split(d_res)
            tall = cat([nh, nl], 1)
            d_mix = dot(cat([d, d], 1), tall, 1, 1)
            d_sys = dot(cat([drh, drh], 1), tall, 1, 1) + dot(drl, nh, 1, 1)
            term = decay * d_mix
            mix_grad = term if mix_grad is None else mix_grad + term
            term = jnp.where(strict, beta * decay * d_sys, 0.0)
            pair_grad = term if pair_grad is None else pair_grad + term
            term = growth * dot(cat([d, d], 1), cat([sh, sl], 1), 1, 1)
            dq = term if dq is None else dq + term
            from_end = to_end * square_product_bt(new, e)
            from_in = (growth * beta) * square_product_bt(d_res, s)
            total = jnp.sum(from_end * kf * rk, axis=0, keepdims=True) + jnp.exp(last) * jnp.sum(
                s * e, axis=0, keepdims=True
            )
            gates.append(jnp.sum(total, axis=1, keepdims=True))
            term = from_end - from_in
            dk = term if dk is None else dk + term
        mh, ml = split(mix_grad * rk_row)
        dq = dq + dot(mh, kr) + dot(ml, kr)
        xh, xl = split(mix_grad * rq)
        dk = dk + dot(xh, qr, 0, 0) + dot(xl, qr, 0, 0)
        gh, gl = split(pair_grad * rk_row)
        dk = dk - (dot(gh, kr) + dot(gl, kr))
        gh, gl = split(pair_grad * rk)
        dk = dk - (dot(gh, kr, 0, 0) + dot(gl, kr, 0, 0))
        along = jnp.sum(qf * dq, axis=1, keepdims=True)
        dq_ref[i] = (rq * (dq - qf * (along / sq))).astype(bf16)
        along = jnp.sum(kf * dk, axis=1, keepdims=True)
        dk_ref[i] = (rk * (dk - kf * (along / sk))).astype(bf16)
    gate_ref[...] = small_ref[...][:, :value_count] + cat(gates, 1)
    for copy in coming:
        copy.wait()


def call(kernel, name, operands, outs, flops, far_ins=(), far_outs=(), scratch=(), limit=VMEM, same=None):
    def spec(n, kind, far):
        space = pltpu.SMEM if kind == jnp.int32 else pltpu.HBM if n in far else pltpu.VMEM
        return pl.BlockSpec(memory_space=space)

    return pl.pallas_call(
        kernel,
        name=name,
        in_specs=[spec(n, x.dtype, far_ins) for n, x in enumerate(operands)],
        out_specs=[spec(n, kind, far_outs) for n, (_, kind) in enumerate(outs)],
        out_shape=[jax.ShapeDtypeStruct(shape, kind) for shape, kind in outs],
        scratch_shapes=list(scratch),
        input_output_aliases=same or {},
        compiler_params=pltpu.CompilerParams(vmem_limit_bytes=limit),
        cost_estimate=pl.CostEstimate(flops=flops, bytes_accessed=1 << 20, transcendentals=0),
    )(*operands)


def turned(parts):
    count = sum(part.shape[1] for part in parts)
    filler = jnp.zeros((parts[0].shape[0], SUB - count), f32)
    return jnp.transpose(cat(parts + [filler], 1))[:count]


def arrange_kernel(nk, nv, *refs):
    store_ref, outs = refs[8], refs[9:-11]
    inputs, made, sems, out_sems = refs[-11:-3], refs[-3], refs[-2], refs[-1]
    held = inputs
    copies = [
        pltpu.make_async_copy(ref, into, sems.at[n]) for n, (ref, into) in enumerate(zip(refs[:8], held))
    ]
    for copy in copies:
        copy.start()
    size = 2 * (nk + nv)
    firsts = (0, nk, 2 * nk, 2 * nk + nv)
    leaving = []
    parts = len(outs)
    copies[0].wait()
    rates = held[0][...]
    heads = rates.shape[0]
    high, low = split(rates)
    rest = (rates - high.astype(f32) - low.astype(f32)).astype(bf16)
    row, column = positions(rates.shape[1])
    before = jnp.where(row <= column, 1.0, 0.0).astype(bf16)
    sums = dot(cat([high, low, rest], 0), before)
    summed = sums[:heads] + sums[heads : 2 * heads] + sums[2 * heads :]
    for n in range(4):
        copies[3 + n].wait()
        ref = held[3 + n]
        count, each, width = ref.shape
        group = each // parts
        for part in range(parts):
            turn = jnp.swapaxes(ref[:, part * group : (part + 1) * group, :].astype(f32), 0, 1)
            here = pl.ds(part * size + firsts[n], group)
            made[here] = turn.astype(bf16)
            leaving.append(
                pltpu.make_async_copy(made.at[here], store_ref.at[here], out_sems.at[n * parts + part])
            )
            leaving[-1].start()
    for n in (1, 2, 7):
        copies[n].wait()
    row, column = positions(heads)
    bias = jnp.sum(jnp.where(row == column, held[1][...], 0.0), axis=1, keepdims=True)
    beta = jax.nn.sigmoid(dot(held[2][...], held[7][...], 1, 1) + bias)
    for part in range(parts):
        first = part * nv
        outs[part][...] = cat([summed[first : first + nv], beta[first : first + nv]], 0)
    for copy in leaving:
        copy.wait()


def part_of(part, store_ref, held, sem):
    size = held.shape[0]
    copy = pltpu.make_async_copy(store_ref.at[pl.ds(part * size, size)], held, sem)
    copy.start()
    return copy


def heads_of(nk, nv, held):
    return [held.at[pl.ds(n, m)] for n, m in ((0, nk), (nk, nk), (2 * nk, nv), (2 * nk + nv, nv))]


def weight_kernel(nv, *refs):
    smalls, (hidden_ref, part_ref, logit_ref) = refs[:-3], refs[-3:]
    rows = [turned([ref[n * SUB : (n + 1) * SUB, nv : 2 * nv] for ref in smalls]) for n in range(smalls[0].shape[0] // SUB)]
    rows = cat(rows, 1)
    logit_ref[...] = rows
    heads = rows.shape[0]
    both = dot(cat(split(rows), 0), hidden_ref[...])
    part_ref[...] = both[:heads] + both[heads:]


def finish_kernel(parts, *refs):
    logit_ref, other_ref, weight_ref, other_weight_ref = refs[:4]
    ins, outs, gate_ref = refs[4 : 4 + 5 * parts], refs[4 + 5 * parts : -8], refs[-8]
    held, wide_ref, sems = refs[-7:-2], refs[-2], refs[-1]
    copies = [
        pltpu.make_async_copy(held[n], outs[n], sems.at[n]) for n in range(5)
    ]
    for n in range(4):
        count, heads, width = held[n].shape
        group = heads // parts
        whole = cat([ref[...].astype(f32) for ref in ins[n * parts : (n + 1) * parts]], 0)
        held[n][...] = jnp.swapaxes(whole, 0, 1).astype(bf16)
        copies[n].start()
        if n == 1:
            high, low = split(cat([logit_ref[...], other_ref[...]], 0))
            weight = cat([weight_ref[...], other_weight_ref[...]], 0)
            held[4][...] = dot(cat([high, low], 0), cat([weight, weight], 0), 0, 0).astype(bf16)
            copies[4].start()
    gates = ins[4 * parts :]
    for n in range(gate_ref.shape[1] // SUB):
        here = slice(n * SUB, (n + 1) * SUB)
        gate_ref[:, here] = turned([ref[here, :] for ref in gates])
    for copy in copies:
        copy.wait()


def exchanged(value, axis, step):
    pairs = [(i, i ^ step) for i in range(lax.axis_size(axis))]
    return value + lax.ppermute(value, axis, pairs)


def on_device(queries, keys_in, values, hidden_in, beta_weight, beta_bias, log_gate, out_grad):
    _, tokens, model_width = hidden_in.shape
    key_heads, key_dim = queries.shape[2:]
    value_heads, value_dim = values.shape[2:]
    nk = KEY_GROUP
    nv = nk * value_heads // key_heads
    parts = key_heads // nk
    count = lax.axis_size("seq")
    place = lax.axis_index("seq").astype(jnp.int32).reshape(1)
    hidden = hidden_in.reshape(tokens, model_width)
    weight = beta_weight.T

    narrow = (nk, tokens, key_dim)
    chunk = (nv, tokens, value_dim)
    state = (nv, key_dim, value_dim)
    moves = (3 * nv, key_dim, value_dim)
    work = nv * 2 * tokens**3
    inputs = (
        log_gate[0].T, beta_bias.reshape(1, value_heads), weight,
        queries[0], keys_in[0], values[0], out_grad[0], hidden,
    )
    size = 2 * (nk + nv)
    stacked = (max(size * parts, STORE // (2 * tokens * key_dim)), tokens, key_dim)
    heads, *rows = call(
        functools.partial(arrange_kernel, nk, nv), "arrange", inputs,
        [(stacked, bf16)] + [((2 * nv, tokens), f32)] * parts,
        work, far_ins=range(len(inputs)), far_outs=(0,), limit=WHOLE,
        scratch=[pltpu.VMEM(x.shape, x.dtype) for x in inputs]
        + [
            pltpu.VMEM((size * parts, tokens, key_dim), bf16),
            pltpu.SemaphoreType.DMA((len(inputs),)), pltpu.SemaphoreType.DMA((4 * parts,)),
        ],
    )
    mine = ((size, tokens, key_dim), bf16)
    length = max(4 * nv * parts, STORE // (2 * tokens * tokens))
    blocks = (length, tokens, tokens)
    stored = ((4 * nv, tokens, tokens), bf16)
    semaphores = pltpu.SemaphoreType.DMA

    def before(part):
        operands = (place, heads, rows[part], *ahead)
        return call(
            functools.partial(before_kernel, part, parts, nk), "before", operands + tuple(store),
            ((blocks, bf16), (moves, f32), (state, f32), mine) + (stored,) * (part == parts - 1),
            60 * work, far_ins=(1,) + (len(operands),) * len(store), far_outs=(0,),
            scratch=[pltpu.VMEM(*stored), semaphores((5,))] + [pltpu.VMEM(*mine)] * (not store),
            same={len(operands): 0} if store else None,
        )

    def relay(stage, hops, operands):
        for hop in hops:
            made = befores[stage - hop]
            operands = operands + ([made[1], arrivals[stage - hop][-1]] if hop else [made[2]])
        if hops == [0]:
            return operands[1]
        (send,) = call(
            functools.partial(relay_kernel, hops, count), "relay", operands, ((state, f32),), work // 4,
        )
        return send

    def new_values(part):
        return call(
            functools.partial(values_kernel, part, parts, nk), "values",
            (place, heads, rows[part], *store, *ahead, *arrivals[part]),
            (
                (chunk, bf16), (chunk, bf16), (chunk, f32), (chunk, f32), (state, f32), (state, f32),
                ((tokens, 2 * nv), f32), mine,
            ) + (stored,) * (part + 1 < parts and part + 1 not in OWN_FETCH),
            20 * work, far_ins=(1, 3),
            scratch=[semaphores((3,))] + [pltpu.VMEM(*stored)] * (part in OWN_FETCH),
        )

    befores, firsts, store, ahead, here = [], [], [], [], place
    arrivals = [[] for _ in range(parts)]
    shift = max(parts, count)
    for stage in range(shift + parts):
        if stage < parts:
            befores.append([*before(stage)])
            store[:] = befores[stage][:1]
            ahead[:] = befores[stage][3:]
            here, befores[stage][2] = lax.optimization_barrier((place, befores[stage][2]))
        elif stage >= shift:
            firsts.append([*new_values(stage - shift)])
            ahead[:] = firsts[-1][7:]
            here, firsts[-1][6] = lax.optimization_barrier((place, firsts[-1][6]))
        due = [hop for hop in range(count - 1) if 0 <= stage - hop < parts]
        due = [hops for hops in ([h for h in due if not h % 2], [h for h in due if h % 2]) if hops]
        sends = [relay(stage, hops, [here]) for hops in due]
        following = stage + 1 if stage + 1 < parts else stage + 1 - shift
        if sends and 0 <= following < parts:
            tied = lax.optimization_barrier((rows[following], *sends))
            rows[following] = tied[0]
            sends = tied[1:]
        for send, hops in zip(sends, due):
            odd = hops[0] % 2
            pairs = [(i, i + 1) for i in range(odd, count - 1, 2)]
            got = lax.ppermute(send, "seq", pairs + [(b, a) for a, b in pairs])
            for hop in hops:
                arrivals[stage - hop].append(got)
    grad_weight, grad_logits = call(
        functools.partial(weight_kernel, nv), "weight", (*[a[6] for a in firsts], hidden),
        (((value_heads, model_width), f32), ((value_heads, tokens), f32)), work // 4,
    )
    here = lax.axis_index("head")
    half = model_width // 2
    swap = [(0, 1), (1, 0)]
    weight_here = lax.dynamic_slice_in_dim(weight, here * half, half, 1)
    weight_there = lax.dynamic_slice_in_dim(weight, (1 - here) * half, half, 1)
    other_weight = lax.ppermute(weight_there, "head", swap)
    other_logits = lax.ppermute(grad_logits, "head", swap)
    seconds = []
    rounds = [
        (axis, 1 << n) for axis in ("dp", "seq") for n in range((lax.axis_size(axis) - 1).bit_length())
    ]
    for part in range(parts):
        _, _, n, r, s, e, small, *_ = firsts[part]
        if part:
            small, grad_weight = lax.optimization_barrier((small, grad_weight))
        for axis, step in rounds[part :] if part == parts - 1 else rounds[part : part + 1]:
            grad_weight = exchanged(grad_weight, axis, step)
        more = part < parts - 1
        seconds.append(
            call(
                functools.partial(keys_kernel, part, parts), "keys",
                (heads, rows[part], *ahead, n, r, s, e, small),
                ((narrow, bf16), (narrow, bf16), ((tokens, nv), f32)) + (mine,) * more,
                20 * work, far_ins=(0,), scratch=[semaphores(())] * more,
            )
        )
        ahead[:] = seconds[-1][3:]
    finals = (
        ((tokens, value_heads, value_dim), bf16), ((tokens, value_heads, value_dim), bf16),
        ((tokens, key_heads, key_dim), bf16), ((tokens, key_heads, key_dim), bf16),
        ((tokens, half), bf16), ((value_heads, tokens), f32),
    )
    attended, grad_values, grad_query, grad_key, grad_hidden, grad_gate = call(
        functools.partial(finish_kernel, parts), "finish",
        (
            grad_logits, other_logits, weight_here, other_weight,
            *[a[0] for a in firsts], *[a[1] for a in firsts],
            *[a[0] for a in seconds], *[a[1] for a in seconds], *[a[2] for a in seconds],
        ),
        finals, work, far_outs=range(5),
        scratch=[pltpu.VMEM(shape, kind) for shape, kind in finals[:5]]
        + [pltpu.VMEM((tokens * value_heads, value_dim), f32), pltpu.SemaphoreType.DMA((5,))],
    )
    return (
        attended[None], grad_query[None], grad_key[None], grad_values[None], grad_gate.T[None],
        grad_hidden[None], grad_weight.T,
    )


def solution(mesh):
    heads = P("dp", "seq", "head", None)
    return jax.shard_map(
        on_device,
        mesh=mesh,
        in_specs=(
            heads, heads, heads, P("dp", "seq", None), P(None, "head"), P("head"),
            P("dp", "seq", "head"), heads,
        ),
        out_specs=(
            heads, heads, heads, heads, P("dp", "seq", "head"), P("dp", "seq", "head"), P(None, "head"),
        ),
        check_vma=False,
    )
```

```python
import functools

import jax
import jax.numpy as jnp
from jax import lax
from jax.experimental import pallas as pl
from jax.experimental.pallas import tpu as pltpu
from jax.sharding import PartitionSpec as P

SUB = 128
KEY_GROUP = 2
OWN_FETCH = (1,)
VMEM = 24 * 1024 * 1024
WHOLE = 56 * 1024 * 1024
STORE = 68 * 1024 * 1024

eps_norm = 1e-06
f32 = jnp.float32
bf16 = jnp.bfloat16


def split(x):
    high = x.astype(bf16)
    return high, (x - high.astype(f32)).astype(bf16)


def dot(a, b, ca=1, cb=0):
    return lax.dot_general(a, b, (((ca,), (cb,)), ((), ())), preferred_element_type=f32)


def cat(parts, axis):
    return jnp.concatenate(parts, axis=axis)


def halves(x):
    width = x.shape[1] // 2
    return x[:, :width] + x[:, width:]


def square_product(a, b):
    ah, al = split(a)
    bh, bl = split(b)
    wide = cat([bh, bl], 1)
    return halves(dot(cat([ah, al], 1), cat([wide, wide], 0)))


def square_product_t(a, b):
    ah, al = split(a)
    bh, bl = split(b)
    wide = cat([bh, bl], 1)
    return halves(dot(cat([ah, al], 0), cat([wide, wide], 0), 0, 0))


def square_product_bt(a, b):
    ah, al = split(a)
    bh, bl = split(b)
    tall = cat([bh, bl], 0)
    return halves(dot(cat([ah, al], 1), cat([tall, tall], 1), 1, 1))


def positions(count):
    shape = (count, count)
    return (lax.broadcasted_iota(jnp.int32, shape, 0), lax.broadcasted_iota(jnp.int32, shape, 1))


def inverses(blocks):
    count = blocks[0].shape[0]
    row, column = positions(count)
    identity = jnp.where(row == column, 1.0, 0.0)
    found = None
    width = 1
    while width < count:
        pairs = (row // (2 * width) == column // (2 * width)) & (row // width != column // width)
        offs = [jnp.where(pairs, block, 0.0) for block in blocks]
        if found is None:
            found = [identity - off for off in offs]
        else:
            firsts = [square_product(inverse, off) for inverse, off in zip(found, offs)]
            found = [
                inverse - square_product(first, inverse) for first, inverse in zip(firsts, found)
            ]
        width *= 2
    return found


def unit_scales(raw, factor):
    data = raw.astype(f32)
    total = jnp.sum(data * data, axis=1, keepdims=True) + eps_norm
    return lax.rsqrt(total) * factor, total


def as_row(column):
    return jnp.transpose(jnp.broadcast_to(column, (column.shape[0], SUB)))[0:1, :]


def chunk_matrices(kr, qr):
    rk, sk = unit_scales(kr, 1.0)
    rq, sq = unit_scales(qr, kr.shape[1] ** (-0.5))
    rk_row = as_row(rk)
    both = dot(cat([kr, qr], 0), kr, 1, 1) * rk_row
    count = kr.shape[0]
    return rk, sk, rq, sq, rk_row, both[:count] * rk, both[count:] * rq


def decay_matrix(g_col, g_row, lower):
    return jnp.exp(jnp.where(lower, g_col - g_row, -1e30))


def before_kernel(part, parts, key_count, place_ref, heads_ref, rows_ref, *refs):
    if part:
        mine_ref = refs[0]
        refs = refs[2:]
    else:
        mine_ref = refs[-1]
        refs = refs[:-1]
    store_ref, m_ref, first_ref, ahead_ref = refs[:4]
    held, sems = refs[-2:]
    value_count = first_ref.shape[0]
    count = mine_ref.shape[1]
    if part == 0:
        part_of(part, heads_ref, mine_ref, sems.at[2]).wait()
    coming = [part_of((part + 1) % parts, heads_ref, ahead_ref, sems.at[3])]
    if part == parts - 1:
        coming.append(part_of(0, store_ref, refs[4], sems.at[4]))
    q_ref, k_ref, v_ref, d_ref = heads_of(key_count, value_count, mine_ref)
    share = value_count // key_count
    row, column = positions(count)
    lower = row >= column
    strict = row > column
    rows = rows_ref[...]
    cols = jnp.transpose(rows)
    scales, mixings, systems = [], [], []
    for i in range(key_count):
        kr, qr = k_ref[i], q_ref[i]
        rk, sk, rq, sq, rk_row, key_key, query_key = chunk_matrices(kr, qr)
        for r in range(share):
            h = i * share + r
            g_col, beta = cols[:, h : h + 1], cols[:, value_count + h : value_count + h + 1]
            decay = decay_matrix(g_col, rows[h : h + 1, :], lower)
            systems.append(jnp.where(strict, beta * decay * key_key, 0.0))
            mixings.append(decay * query_key)
            scales.append((rk, rq, beta, g_col))
    pieces = count // SUB
    diagonal = []
    for a in systems:
        for n in range(pieces):
            diagonal.append(a[n * SUB : (n + 1) * SUB, n * SUB : (n + 1) * SUB])
    diagonal = inverses(diagonal)
    identity = jnp.where(positions(SUB)[0] == positions(SUB)[1], 1.0, 0.0)
    copies = []

    def leave(n):
        size = 2 * value_count
        here = pl.ds(n * size, size)
        there = pl.ds((2 * part + n) * size, size)
        copies.append(pltpu.make_async_copy(held.at[here], store_ref.at[there], sems.at[n]))
        copies[-1].start()

    for h in range(value_count):
        a = systems[h]
        blocks = [[None] * pieces for _ in range(pieces)]
        for n in range(pieces):
            blocks[n][n] = diagonal[h * pieces + n]
            for m in range(n):
                total = None
                for l in range(m, n):
                    term = square_product(
                        a[n * SUB : (n + 1) * SUB, l * SUB : (l + 1) * SUB], blocks[l][m]
                    )
                    total = term if total is None else total + term
                blocks[n][m] = -square_product(blocks[n][n], total)
            for m in range(n + 1, pieces):
                blocks[n][m] = jnp.zeros((SUB, SUB), f32)
        held[h], held[value_count + h] = split(cat([cat(line, 1) for line in blocks], 0))
    leave(0)
    for h in range(value_count):
        rk, rq, beta, g_col = scales[h]
        kr, qr, v, d = k_ref[h // share], q_ref[h // share], v_ref[h], d_ref[h]
        width = kr.shape[1]
        last = g_col[count - 1 : count, :]
        growth = jnp.exp(g_col)
        to_end = jnp.exp(last - g_col) * rk
        ph, pl_ = split(mixings[h])
        pulled = dot(ph, d, 0, 0) + dot(pl_, d, 0, 0)
        th, tl = held[h], held[value_count + h]
        keys_h, keys_l = split(to_end * kr.astype(f32))
        pull_h, pull_l = split(pulled)
        high = dot(th, cat([keys_h, pull_h, keys_l, pull_l], 1), 0, 0)
        yz = high[:, : 2 * width] + high[:, 2 * width :]
        yz = yz + dot(tl, cat([keys_h, pull_h], 1), 0, 0)
        y, z = yz[:, :width], yz[:, width:]
        held[2 * value_count + h], held[3 * value_count + h] = split(yz)
        yb = y * beta
        bh, bl = split(yb)
        base = dot(bh, v, 0, 0) + dot(bl, v, 0, 0)
        mh, ml = split(yb * (growth * rk))
        m_ref[h] = identity * jnp.exp(last) - (dot(mh, kr, 0, 0) + dot(ml, kr, 0, 0))
        outs_h, outs_l = split((growth * rq) * d.astype(f32))
        ins_h, ins_l = split((beta * growth * rk) * z)
        push = halves(
            dot(qr, cat([outs_h, outs_l], 1), 0, 0) - dot(kr, cat([ins_h, ins_l], 1), 0, 0)
        )
        m_ref[value_count + h] = base
        m_ref[2 * value_count + h] = push
        first_ref[h] = jnp.where(place_ref[0] == 0, base, push)
    leave(1)
    for copy in copies + coming:
        copy.wait()


def relay_kernel(hops, count, place_ref, *refs):
    place, out_ref = place_ref[0], refs[-1]
    at = 0
    for hop in hops:
        if hop == 0:
            first_ref = refs[at]
            at += 1

            @pl.when((place == 0) | (place == count - 1))
            def _():
                out_ref[...] = first_ref[...]

            continue
        parts_ref, got_ref = refs[at : at + 2]
        heads = got_ref.shape[0]
        at += 2

        @pl.when(place == hop)
        def _():
            for h in range(heads):
                out_ref[h] = square_product(parts_ref[h], got_ref[h]) + parts_ref[heads + h]

        @pl.when(place == count - 1 - hop)
        def _():
            for h in range(heads):
                out_ref[h] = square_product_t(parts_ref[h], got_ref[h]) + parts_ref[2 * heads + h]


def chosen(place, arrivals, h, first, step):
    total = jnp.zeros(arrivals[0].shape[1:], f32)
    for hop, arrival in enumerate(arrivals):
        total = jnp.where(first + step * place == hop, arrival[h], total)
    return total


def values_kernel(part, parts, key_count, *refs):
    place_ref, heads_ref, rows_ref, store_ref, mine_ref = refs[:5]
    own, other = part in OWN_FETCH, part + 1 < parts and part + 1 not in OWN_FETCH
    if own:
        held, refs = refs[-1], refs[5:-1]
    else:
        held, refs = refs[5], refs[6:]
    last = part == parts - 1
    outs = 9 if other else 7 if last else 8
    arrivals = refs[: -outs - 1]
    o_ref, dv_ref, n_ref, r_ref, s_ref, e_ref, small_ref = refs[-outs - 1 :][:7]
    sems = refs[-1]
    value_count, count, width = o_ref.shape
    if own:
        fetched = part_of(part, store_ref, held, sems.at[2])
    coming = [] if last else [part_of(part + 1, heads_ref, refs[6 - outs], sems.at[0])]
    if other:
        coming.append(part_of(part + 1, store_ref, refs[-2], sems.at[1]))
    q_ref, k_ref, v_ref, d_ref = heads_of(key_count, value_count, mine_ref)
    share = value_count // key_count
    row, column = positions(count)
    lower = row >= column
    rows = rows_ref[...]
    cols = jnp.transpose(rows)
    place = place_ref[0]
    ready = []
    for i in range(key_count):
        kr, qr = k_ref[i], q_ref[i]
        rk, _ = unit_scales(kr, 1.0)
        rq, _ = unit_scales(qr, width ** (-0.5))
        query_key = dot(qr, kr, 1, 1) * as_row(rk) * rq
        both = cat([qr, kr], 0)
        for r in range(share):
            h = i * share + r
            g_col, beta = cols[:, h : h + 1], cols[:, value_count + h : value_count + h + 1]
            decay = decay_matrix(g_col, rows[h : h + 1, :], lower)
            growth = jnp.exp(g_col)
            s = chosen(place, arrivals, h, -1, 1)
            e = chosen(place, arrivals, h, len(arrivals) - 1, -1)
            s_ref[h] = s
            e_ref[h] = e
            carried = halves(dot(both, cat(split(s), 1)))
            residual = beta * (v_ref[h].astype(f32) - (growth * rk) * carried[count:])
            ready.append(
                (split(residual), split(decay * query_key), (growth * rq) * carried[:count], beta, split(e))
            )
    if own:
        fetched.wait()
    gates, logits = [], []
    for h, ((rh, rl), (ph, pl_), from_state, beta, (eh, el)) in enumerate(ready):
        th, tl = held[h], held[value_count + h]
        yzh, yzl = held[2 * value_count + h], held[3 * value_count + h]
        new = halves(dot(th, cat([rh, rl], 1))) + dot(tl, rh)
        n_ref[h] = new
        nh, nl = split(new)
        out = from_state + halves(dot(ph, cat([nh, nl], 1))) + dot(pl_, nh)
        o_ref[h] = out.astype(bf16)
        wide = cat([eh, el], 1)
        pulled = halves(dot(cat([yzh[:, :width], yzl[:, :width]], 1), cat([wide, wide], 0)))
        d_res = yzh[:, width:].astype(f32) + yzl[:, width:].astype(f32) + pulled
        r_ref[h] = d_res
        dv = beta * d_res
        dv_ref[h] = dv.astype(bf16)
        logits.append((1.0 - beta) * jnp.sum(d_res * new, axis=1, keepdims=True))
        gates.append(
            jnp.sum(d_ref[h].astype(f32) * out - dv * v_ref[h].astype(f32), axis=1, keepdims=True)
        )
    after = jnp.where(row <= column, 1.0, 0.0).astype(bf16)
    gh, gl = split(cat(gates, 1))
    small_ref[...] = cat([halves(dot(after, cat([gh, gl], 1)))] + logits, 1)
    for copy in coming:
        copy.wait()


def keys_kernel(
    rows_ref, mine_ref, n_ref, r_ref, s_ref, e_ref, small_ref,
    dq_ref, dk_ref, gate_ref,
):
    key_count, count, width = dq_ref.shape
    value_count = n_ref.shape[0]
    q_ref, k_ref, _, d_ref = heads_of(key_count, value_count, mine_ref)
    share = value_count // key_count
    row, column = positions(count)
    lower = row >= column
    strict = row > column
    rows = rows_ref[...]
    cols = jnp.transpose(rows)
    gates = []
    for i in range(key_count):
        kr, qr = k_ref[i], q_ref[i]
        kf, qf = kr.astype(f32), qr.astype(f32)
        rk, sk = unit_scales(kr, 1.0)
        rq, sq = unit_scales(qr, width ** (-0.5))
        rk_row = as_row(rk)
        mix_grad = pair_grad = dq = dk = None
        for r in range(share):
            h = i * share + r
            g_col, beta = cols[:, h : h + 1], cols[:, value_count + h : value_count + h + 1]
            decay = decay_matrix(g_col, rows[h : h + 1, :], lower)
            growth = jnp.exp(g_col)
            last = g_col[count - 1 : count, :]
            to_end = jnp.exp(last - g_col)
            d = d_ref[h]
            s, e, new, d_res = s_ref[h], e_ref[h], n_ref[h], r_ref[h]
            sh, sl = split(s)
            nh, nl = split(new)
            drh, drl = split(d_res)
            tall = cat([nh, nl], 1)
            d_mix = dot(cat([d, d], 1), tall, 1, 1)
            d_sys = dot(cat([drh, drh], 1), tall, 1, 1) + dot(drl, nh, 1, 1)
            term = decay * d_mix
            mix_grad = term if mix_grad is None else mix_grad + term
            term = jnp.where(strict, beta * decay * d_sys, 0.0)
            pair_grad = term if pair_grad is None else pair_grad + term
            term = growth * dot(cat([d, d], 1), cat([sh, sl], 1), 1, 1)
            dq = term if dq is None else dq + term
            from_end = to_end * square_product_bt(new, e)
            from_in = (growth * beta) * square_product_bt(d_res, s)
            total = jnp.sum(from_end * kf * rk, axis=0, keepdims=True) + jnp.exp(last) * jnp.sum(
                s * e, axis=0, keepdims=True
            )
            gates.append(jnp.sum(total, axis=1, keepdims=True))
            term = from_end - from_in
            dk = term if dk is None else dk + term
        mh, ml = split(mix_grad * rk_row)
        dq = dq + dot(mh, kr) + dot(ml, kr)
        xh, xl = split(mix_grad * rq)
        dk = dk + dot(xh, qr, 0, 0) + dot(xl, qr, 0, 0)
        gh, gl = split(pair_grad * rk_row)
        dk = dk - (dot(gh, kr) + dot(gl, kr))
        gh, gl = split(pair_grad * rk)
        dk = dk - (dot(gh, kr, 0, 0) + dot(gl, kr, 0, 0))
        along = jnp.sum(qf * dq, axis=1, keepdims=True)
        dq_ref[i] = (rq * (dq - qf * (along / sq))).astype(bf16)
        along = jnp.sum(kf * dk, axis=1, keepdims=True)
        dk_ref[i] = (rk * (dk - kf * (along / sk))).astype(bf16)
    gate_ref[...] = small_ref[...][:, :value_count] + cat(gates, 1)


def call(kernel, name, operands, outs, flops, far_ins=(), far_outs=(), scratch=(), limit=VMEM, same=None):
    def spec(n, kind, far):
        space = pltpu.SMEM if kind == jnp.int32 else pltpu.HBM if n in far else pltpu.VMEM
        return pl.BlockSpec(memory_space=space)

    return pl.pallas_call(
        kernel,
        name=name,
        in_specs=[spec(n, x.dtype, far_ins) for n, x in enumerate(operands)],
        out_specs=[spec(n, kind, far_outs) for n, (_, kind) in enumerate(outs)],
        out_shape=[jax.ShapeDtypeStruct(shape, kind) for shape, kind in outs],
        scratch_shapes=list(scratch),
        input_output_aliases=same or {},
        compiler_params=pltpu.CompilerParams(vmem_limit_bytes=limit),
        cost_estimate=pl.CostEstimate(flops=flops, bytes_accessed=1 << 20, transcendentals=0),
    )(*operands)


def turned(parts):
    count = sum(part.shape[1] for part in parts)
    filler = jnp.zeros((parts[0].shape[0], SUB - count), f32)
    return jnp.transpose(cat(parts + [filler], 1))[:count]


def arrange_kernel(nk, nv, *refs):
    store_ref, outs = refs[8], refs[9:-11]
    inputs, made, sems, out_sems = refs[-11:-3], refs[-3], refs[-2], refs[-1]
    held = inputs
    copies = [
        pltpu.make_async_copy(ref, into, sems.at[n]) for n, (ref, into) in enumerate(zip(refs[:8], held))
    ]
    for copy in copies:
        copy.start()
    size = 2 * (nk + nv)
    firsts = (0, nk, 2 * nk, 2 * nk + nv)
    leaving = []
    parts = len(outs)
    copies[0].wait()
    rates = held[0][...]
    heads = rates.shape[0]
    high, low = split(rates)
    rest = (rates - high.astype(f32) - low.astype(f32)).astype(bf16)
    row, column = positions(rates.shape[1])
    before = jnp.where(row <= column, 1.0, 0.0).astype(bf16)
    sums = dot(cat([high, low, rest], 0), before)
    summed = sums[:heads] + sums[heads : 2 * heads] + sums[2 * heads :]
    for n in range(4):
        copies[3 + n].wait()
        ref = held[3 + n]
        count, each, width = ref.shape
        group = each // parts
        for part in range(parts):
            turn = jnp.swapaxes(ref[:, part * group : (part + 1) * group, :].astype(f32), 0, 1)
            here = pl.ds(part * size + firsts[n], group)
            made[here] = turn.astype(bf16)
            leaving.append(
                pltpu.make_async_copy(made.at[here], store_ref.at[here], out_sems.at[n * parts + part])
            )
            leaving[-1].start()
    for n in (1, 2, 7):
        copies[n].wait()
    row, column = positions(heads)
    bias = jnp.sum(jnp.where(row == column, held[1][...], 0.0), axis=1, keepdims=True)
    beta = jax.nn.sigmoid(dot(held[2][...], held[7][...], 1, 1) + bias)
    for part in range(parts):
        first = part * nv
        outs[part][...] = cat([summed[first : first + nv], beta[first : first + nv]], 0)
    for copy in leaving:
        copy.wait()


def part_of(part, store_ref, held, sem):
    size = held.shape[0]
    copy = pltpu.make_async_copy(store_ref.at[pl.ds(part * size, size)], held, sem)
    copy.start()
    return copy


def heads_of(nk, nv, held):
    return [held.at[pl.ds(n, m)] for n, m in ((0, nk), (nk, nk), (2 * nk, nv), (2 * nk + nv, nv))]


def weight_kernel(nv, *refs):
    smalls, (hidden_ref, part_ref, logit_ref) = refs[:-3], refs[-3:]
    rows = [turned([ref[n * SUB : (n + 1) * SUB, nv : 2 * nv] for ref in smalls]) for n in range(smalls[0].shape[0] // SUB)]
    rows = cat(rows, 1)
    logit_ref[...] = rows
    heads = rows.shape[0]
    both = dot(cat(split(rows), 0), hidden_ref[...])
    part_ref[...] = both[:heads] + both[heads:]


def finish_kernel(parts, *refs):
    logit_ref, other_ref, weight_ref, other_weight_ref = refs[:4]
    ins, outs, gate_ref = refs[4 : 4 + 5 * parts], refs[4 + 5 * parts : -8], refs[-8]
    held, wide_ref, sems = refs[-7:-2], refs[-2], refs[-1]
    copies = [
        pltpu.make_async_copy(held[n], outs[n], sems.at[n]) for n in range(5)
    ]
    for n in range(4):
        count, heads, width = held[n].shape
        group = heads // parts
        whole = cat([ref[...].astype(f32) for ref in ins[n * parts : (n + 1) * parts]], 0)
        held[n][...] = jnp.swapaxes(whole, 0, 1).astype(bf16)
        copies[n].start()
        if n == 1:
            high, low = split(cat([logit_ref[...], other_ref[...]], 0))
            weight = cat([weight_ref[...], other_weight_ref[...]], 0)
            held[4][...] = dot(cat([high, low], 0), cat([weight, weight], 0), 0, 0).astype(bf16)
            copies[4].start()
    gates = ins[4 * parts :]
    for n in range(gate_ref.shape[1] // SUB):
        here = slice(n * SUB, (n + 1) * SUB)
        gate_ref[:, here] = turned([ref[here, :] for ref in gates])
    for copy in copies:
        copy.wait()


def exchanged(value, axis, step):
    pairs = [(i, i ^ step) for i in range(lax.axis_size(axis))]
    return value + lax.ppermute(value, axis, pairs)


def on_device(queries, keys_in, values, hidden_in, beta_weight, beta_bias, log_gate, out_grad):
    _, tokens, model_width = hidden_in.shape
    key_heads, key_dim = queries.shape[2:]
    value_heads, value_dim = values.shape[2:]
    nk = KEY_GROUP
    nv = nk * value_heads // key_heads
    parts = key_heads // nk
    count = lax.axis_size("seq")
    place = lax.axis_index("seq").astype(jnp.int32).reshape(1)
    hidden = hidden_in.reshape(tokens, model_width)
    weight = beta_weight.T

    narrow = (nk, tokens, key_dim)
    chunk = (nv, tokens, value_dim)
    state = (nv, key_dim, value_dim)
    moves = (3 * nv, key_dim, value_dim)
    work = nv * 2 * tokens**3
    inputs = (
        log_gate[0].T, beta_bias.reshape(1, value_heads), weight,
        queries[0], keys_in[0], values[0], out_grad[0], hidden,
    )
    size = 2 * (nk + nv)
    stacked = (max(size * parts, STORE // (2 * tokens * key_dim)), tokens, key_dim)
    heads, *rows = call(
        functools.partial(arrange_kernel, nk, nv), "arrange", inputs,
        [(stacked, bf16)] + [((2 * nv, tokens), f32)] * parts,
        work, far_ins=range(len(inputs)), far_outs=(0,), limit=WHOLE,
        scratch=[pltpu.VMEM(x.shape, x.dtype) for x in inputs]
        + [
            pltpu.VMEM((size * parts, tokens, key_dim), bf16),
            pltpu.SemaphoreType.DMA((len(inputs),)), pltpu.SemaphoreType.DMA((4 * parts,)),
        ],
    )
    mine = ((size, tokens, key_dim), bf16)
    length = max(4 * nv * parts, STORE // (2 * tokens * tokens))
    blocks = (length, tokens, tokens)
    stored = ((4 * nv, tokens, tokens), bf16)
    semaphores = pltpu.SemaphoreType.DMA

    def before(part):
        operands = (place, heads, rows[part], *ahead)
        return call(
            functools.partial(before_kernel, part, parts, nk), "before", operands + tuple(store),
            ((blocks, bf16), (moves, f32), (state, f32), mine) + (stored,) * (part == parts - 1),
            60 * work, far_ins=(1,) + (len(operands),) * len(store), far_outs=(0,),
            scratch=[pltpu.VMEM(*stored), semaphores((5,))] + [pltpu.VMEM(*mine)] * (not store),
            same={len(operands): 0} if store else None,
        )

    def relay(stage, hops, operands):
        for hop in hops:
            made = befores[stage - hop]
            operands = operands + ([made[1], arrivals[stage - hop][-1]] if hop else [made[2]])
        if hops == [0]:
            return operands[1]
        (send,) = call(
            functools.partial(relay_kernel, hops, count), "relay", operands, ((state, f32),), work // 4,
        )
        return send

    def new_values(part):
        return call(
            functools.partial(values_kernel, part, parts, nk), "values",
            (place, heads, rows[part], *store, *ahead, *arrivals[part]),
            (
                (chunk, bf16), (chunk, bf16), (chunk, f32), (chunk, f32), (state, f32), (state, f32),
                ((tokens, 2 * nv), f32),
            ) + (mine,) * (part + 1 < parts) + (stored,) * (part + 1 < parts and part + 1 not in OWN_FETCH),
            20 * work, far_ins=(1, 3),
            scratch=[semaphores((3,))] + [pltpu.VMEM(*stored)] * (part in OWN_FETCH),
        )

    befores, firsts, store, ahead, mines, here = [], [], [], [], [], place
    arrivals = [[] for _ in range(parts)]
    shift = max(parts, count)
    for stage in range(shift + parts):
        if stage < parts:
            befores.append([*before(stage)])
            store[:] = befores[stage][:1]
            ahead[:] = befores[stage][3:]
            here, befores[stage][2] = lax.optimization_barrier((place, befores[stage][2]))
        elif stage >= shift:
            mines.append(ahead[0])
            firsts.append([*new_values(stage - shift)])
            ahead[:] = firsts[-1][7:]
            here, firsts[-1][6] = lax.optimization_barrier((place, firsts[-1][6]))
        due = [hop for hop in range(count - 1) if 0 <= stage - hop < parts]
        due = [hops for hops in ([h for h in due if not h % 2], [h for h in due if h % 2]) if hops]
        sends = [relay(stage, hops, [here]) for hops in due]
        following = stage + 1 if stage + 1 < parts else stage + 1 - shift
        if sends and 0 <= following < parts:
            tied = lax.optimization_barrier((rows[following], *sends))
            rows[following] = tied[0]
            sends = tied[1:]
        for send, hops in zip(sends, due):
            odd = hops[0] % 2
            pairs = [(i, i + 1) for i in range(odd, count - 1, 2)]
            got = lax.ppermute(send, "seq", pairs + [(b, a) for a, b in pairs])
            for hop in hops:
                arrivals[stage - hop].append(got)
    grad_weight, grad_logits = call(
        functools.partial(weight_kernel, nv), "weight", (*[a[6] for a in firsts], hidden),
        (((value_heads, model_width), f32), ((value_heads, tokens), f32)), work // 4,
    )
    here = lax.axis_index("head")
    half = model_width // 2
    swap = [(0, 1), (1, 0)]
    weight_here = lax.dynamic_slice_in_dim(weight, here * half, half, 1)
    weight_there = lax.dynamic_slice_in_dim(weight, (1 - here) * half, half, 1)
    other_weight = lax.ppermute(weight_there, "head", swap)
    other_logits = lax.ppermute(grad_logits, "head", swap)
    seconds = []
    rounds = [
        (axis, 1 << n) for axis in ("dp", "seq") for n in range((lax.axis_size(axis) - 1).bit_length())
    ]
    for part in range(parts):
        _, _, n, r, s, e, small, *_ = firsts[part]
        if part:
            small, grad_weight = lax.optimization_barrier((small, grad_weight))
        for axis, step in rounds[part :] if part == parts - 1 else rounds[part : part + 1]:
            grad_weight = exchanged(grad_weight, axis, step)
        seconds.append(
            call(
                keys_kernel, "keys", (rows[part], mines[part], n, r, s, e, small),
                ((narrow, bf16), (narrow, bf16), ((tokens, nv), f32)), 20 * work,
            )
        )
    finals = (
        ((tokens, value_heads, value_dim), bf16), ((tokens, value_heads, value_dim), bf16),
        ((tokens, key_heads, key_dim), bf16), ((tokens, key_heads, key_dim), bf16),
        ((tokens, half), bf16), ((value_heads, tokens), f32),
    )
    attended, grad_values, grad_query, grad_key, grad_hidden, grad_gate = call(
        functools.partial(finish_kernel, parts), "finish",
        (
            grad_logits, other_logits, weight_here, other_weight,
            *[a[0] for a in firsts], *[a[1] for a in firsts],
            *[a[0] for a in seconds], *[a[1] for a in seconds], *[a[2] for a in seconds],
        ),
        finals, work, far_outs=range(5),
        scratch=[pltpu.VMEM(shape, kind) for shape, kind in finals[:5]]
        + [pltpu.VMEM((tokens * value_heads, value_dim), f32), pltpu.SemaphoreType.DMA((5,))],
    )
    return (
        attended[None], grad_query[None], grad_key[None], grad_values[None], grad_gate.T[None],
        grad_hidden[None], grad_weight.T,
    )


def solution(mesh):
    heads = P("dp", "seq", "head", None)
    return jax.shard_map(
        on_device,
        mesh=mesh,
        in_specs=(
            heads, heads, heads, P("dp", "seq", None), P(None, "head"), P("head"),
            P("dp", "seq", "head"), heads,
        ),
        out_specs=(
            heads, heads, heads, heads, P("dp", "seq", "head"), P("dp", "seq", "head"), P(None, "head"),
        ),
        check_vma=False,
    )
```
